512 devices in a mesh: outer: 4 (over x), shard: 4 (over z_hi, core), tensor: 32 (over y, z_lo).
Axes of the slice: x: 4, y: 4, z: 16 (z_hi: 2, z_lo: 8; z = z_hi * 8 + z_lo), core: 2. Of those that a mesh axis runs over, the one named last changes fastest.
Arguments:
- quantized: bfloat16 [2048, 4096], P(('outer', 'shard'), 'tensor'), may hold values from -6 to 6
- scales: float32 [2048, 32], P(('outer', 'shard'), 'tensor'), may hold values from 0.3 to 3
- d_hidden: bfloat16 [2048, 16384], P(('outer', 'shard'), 'tensor'), may hold values from -6 to 6
- w_gate: bfloat16 [4096, 16384], P('shard', 'tensor'), may hold values from -0.09375 to 0.09375
- w_up: bfloat16 [4096, 16384], P('shard', 'tensor'), may hold values from -0.09375 to 0.09375
Outputs:
- d_input: bfloat16 [2048, 4096], P(('outer', 'shard'), 'tensor')
- d_gate_weight: bfloat16 [4096, 16384], P('shard', 'tensor')
- d_up_weight: bfloat16 [4096, 16384], P('shard', 'tensor')
The draws below stay inside these ranges and needn't reach their ends.
All inputs are finite; a program needn't handle non-finite values.
Results may differ from the reference program's by a relative error of at most 0.03.
Values may be sent and summed in bfloat16 or wider, within the bound.
No kernel may reach another device: no remote copies, remote signals or barrier semaphores. Data moves between devices by JAX's collectives and lax.ppermute only.
A program may use at most 64 MiB of HBM per device.

```python
import math
import jax
import jax.numpy as jnp

D = 4096
FF = 16384
BLOCK = 128
TOKENS = 2048


def steps_of(own_key, shape, pieces, low, high):
    gain = 1.0
    for position, shards_of in pieces:
        steps = jax.random.uniform(jax.random.fold_in(jax.random.fold_in(own_key, 6), position), (shards_of,), jnp.float32, low / len(pieces), high / len(pieces))
        gain = gain * jnp.repeat(jnp.exp(steps), shape[position] // shards_of).reshape((-1,) + (1,) * (len(shape) - 1 - position))
    return gain


def centred(stream_key, dims, width, bound, pieces=(), held_as=jnp.bfloat16):
    result = width * jax.random.normal(stream_key, dims, jnp.float32)
    if pieces:
        result = result * steps_of(stream_key, dims, pieces, -0.22, 0.18)
    return jnp.clip(result, -bound, bound).astype(held_as)


def setup_inputs(seed: int = 0) -> dict:
    arg_keys = jax.random.split(jax.random.key(seed), 6)
    quantized = centred(arg_keys[0], (TOKENS, D), 1.0, 6.0, ((0, 16), (1, 32)))
    scales = jnp.clip(jnp.exp(math.log(3.0) - 2.3025851 * jax.random.uniform(arg_keys[1], (TOKENS, D // BLOCK), jnp.float32) ** steps_of(arg_keys[1], (TOKENS, D // BLOCK), ((0, 16), (1, 32)), -0.2, 0.2)), 0.3, 3.0)
    d_hidden = centred(arg_keys[2], (TOKENS, FF), 1.0, 6.0, ((0, 16), (1, 32)))
    w_gate = centred(arg_keys[3], (D, FF), D ** -0.5, 0.09375, ((0, 4), (1, 32)))
    w_up = centred(arg_keys[4], (D, FF), D ** -0.5, 0.09375, ((0, 4), (1, 32)))
    return {"quantized": quantized, "scales": scales, "d_hidden": d_hidden, "w_gate": w_gate, "w_up": w_up}


def reference(quantized, scales, d_hidden, w_gate, w_up):
    count = quantized.shape[0]
    blocks = scales.shape[1]
    inputs = (quantized.astype(jnp.float32).reshape(count, blocks, BLOCK) * scales[:, :, None]).reshape(count, D).astype(jnp.bfloat16)
    gate = jnp.dot(inputs, w_gate, preferred_element_type=jnp.float32)
    up = jnp.dot(inputs, w_up, preferred_element_type=jnp.float32)
    sig = jax.nn.sigmoid(gate)
    grad_out = d_hidden.astype(jnp.float32)
    d_gate = (grad_out * up * sig * (1.0 + gate * (1.0 - sig))).astype(jnp.bfloat16)
    d_up = (grad_out * gate * sig).astype(jnp.bfloat16)
    d_input = jnp.dot(d_gate, w_gate.T, preferred_element_type=jnp.float32) + jnp.dot(d_up, w_up.T, preferred_element_type=jnp.float32)
    d_gate_weight = jnp.dot(inputs.T, d_gate, preferred_element_type=jnp.float32)
    d_up_weight = jnp.dot(inputs.T, d_up, preferred_element_type=jnp.float32)
    return d_input.astype(jnp.bfloat16), d_gate_weight.astype(jnp.bfloat16), d_up_weight.astype(jnp.bfloat16)
```

```python
import jax
import jax.numpy as jnp
import numpy as np
from jax import lax
from jax.sharding import Mesh, PartitionSpec as P

AXES = ("x", "zh", "c", "y", "zl")
SIZES = {"x": 4, "zh": 2, "c": 2, "y": 4, "zl": 8}
ROWS = ("x", "zh", "c")
COLS = ("y", "zl")
SHARD = ("zh", "c")
F32 = jnp.float32
BF16 = jnp.bfloat16


def permute(value, axes, target):
    sizes = [SIZES[a] for a in axes]
    pairs = []
    for i in range(int(np.prod(sizes))):
        at = dict(zip(axes, map(int, np.unravel_index(i, sizes))))
        to = target(at)
        pairs.append((i, int(np.ravel_multi_index([to[a] for a in axes], sizes))))
    return lax.ppermute(value, axes if len(axes) > 1 else axes[0], pairs)


def swap_shard_y(value):
    return permute(
        value,
        ("zh", "c", "y"),
        lambda d: {"zh": d["y"] // 2, "c": d["y"] % 2, "y": d["zh"] * 2 + d["c"]},
    )


def swap_core(value):
    return permute(value, ("c",), lambda d: {"c": 1 - d["c"]})


def swap_half(value):
    return permute(value, ("zh",), lambda d: {"zh": 1 - d["zh"]})


def spread(value, axis):
    n = SIZES[axis]
    return lax.all_to_all(jnp.broadcast_to(value[None], (n,) + value.shape), axis, 0, 0)


def relative(blocks):
    s = lax.axis_index("zh") * 2 + lax.axis_index("c")
    return jnp.stack([lax.dynamic_index_in_dim(blocks, s ^ r, 0, keepdims=False) for r in range(4)])


def shards(quantized, scales, d_hidden, w_gate, w_up):
    count, width = quantized.shape
    ff = w_gate.shape[1]
    rows = w_gate.shape[0]
    local = (quantized.astype(F32) * scales).astype(BF16)
    with jax.named_scope("gather_inputs"):
        held = spread(swap_shard_y(local), "zl")
        held = held.transpose(1, 0, 2).reshape(count, rows)
        held = spread(held, "y")
        inputs = relative(held)
    with jax.named_scope("partial_gate_up"):
        w = jnp.concatenate([w_gate, w_up], axis=1)
        parts = jnp.dot(inputs.reshape(4 * count, rows), w, preferred_element_type=F32)
        parts = parts.reshape(2, 2, count, 2 * ff)
    with jax.named_scope("core_sum"):
        parts = parts[:, 0] + swap_core(parts[:, 1].astype(BF16)).astype(F32)
    with jax.named_scope("half_sum"):
        pre = parts[0] + swap_half(parts[1].astype(BF16)).astype(F32)
    with jax.named_scope("elementwise"):
        gate, up = pre[:, :ff], pre[:, ff:]
        sig = jax.nn.sigmoid(gate)
        grad_out = d_hidden.astype(F32)
        d_gate = (grad_out * up * sig * (1.0 + gate * (1.0 - sig))).astype(BF16)
        d_up = (grad_out * gate * sig).astype(BF16)
        d = jnp.concatenate([d_gate, d_up], axis=1)
    with jax.named_scope("d_half"):
        d = jnp.stack([d, swap_half(d)])
    with jax.named_scope("d_core"):
        d = jnp.stack([d, swap_core(d)], axis=1)
    d = d.reshape(4 * count, 2 * ff)
    with jax.named_scope("weight_grads"):
        dw = jnp.dot(inputs.reshape(4 * count, rows).T, d, preferred_element_type=F32).astype(BF16)
        dw = lax.psum(dw, "x")
    with jax.named_scope("d_input"):
        di = lax.dot_general(d, w, (((1,), (1,)), ((), ())), preferred_element_type=F32).astype(BF16)
        di = relative(di.reshape(4, count, rows))
        di = jnp.sum(lax.all_to_all(di, "y", 0, 0).astype(F32), axis=0).astype(BF16)
        di = di.reshape(count, 8, width).transpose(1, 0, 2)
        di = jnp.sum(lax.all_to_all(di, "zl", 0, 0).astype(F32), axis=0).astype(BF16)
        di = swap_shard_y(di)
    return di, dw[:, :ff], dw[:, ff:]


def solution(mesh):
    fine = Mesh(mesh.devices.reshape([SIZES[a] for a in AXES]), AXES)
    in_specs = (P(ROWS, COLS), P(ROWS, COLS), P(ROWS, COLS), P(SHARD, COLS), P(SHARD, COLS))
    out_specs = (P(ROWS, COLS), P(SHARD, COLS), P(SHARD, COLS))
    return jax.shard_map(shards, mesh=fine, in_specs=in_specs, out_specs=out_specs, check_vma=False)
```

```python
import jax
import jax.numpy as jnp
import numpy as np
from jax import lax
from jax.sharding import Mesh, PartitionSpec as P

AXES = ("x", "zh", "c", "y", "zl")
SIZES = {"x": 4, "zh": 2, "c": 2, "y": 4, "zl": 8}
ROWS = ("x", "zh", "c")
COLS = ("y", "zl")
SHARD = ("zh", "c")
F32 = jnp.float32
BF16 = jnp.bfloat16


def permute(value, axes, target):
    sizes = [SIZES[a] for a in axes]
    pairs = []
    for i in range(int(np.prod(sizes))):
        at = dict(zip(axes, map(int, np.unravel_index(i, sizes))))
        to = target(at)
        pairs.append((i, int(np.ravel_multi_index([to[a] for a in axes], sizes))))
    return lax.ppermute(value, axes if len(axes) > 1 else axes[0], pairs)


def swap_shard_y(value):
    return permute(
        value,
        ("zh", "c", "y"),
        lambda d: {"zh": d["y"] // 2, "c": d["y"] % 2, "y": d["zh"] * 2 + d["c"]},
    )


def swap_core(value):
    return permute(value, ("c",), lambda d: {"c": 1 - d["c"]})


def swap_half(value):
    return permute(value, ("zh",), lambda d: {"zh": 1 - d["zh"]})


def spread(value, axis):
    n = SIZES[axis]
    return lax.all_to_all(jnp.broadcast_to(value[None], (n,) + value.shape), axis, 0, 0)


def relative(blocks):
    zh, c = lax.axis_index("zh"), lax.axis_index("c")
    picks = [(zh ^ r_zh) * 2 + (c ^ r_c) for r_c in range(2) for r_zh in range(2)]
    return jnp.stack([lax.dynamic_index_in_dim(blocks, p, 0, keepdims=False) for p in picks])


def absolute(blocks):
    zh, c = lax.axis_index("zh"), lax.axis_index("c")
    picks = [(c ^ c_to) * 2 + (zh ^ zh_to) for zh_to in range(2) for c_to in range(2)]
    return jnp.stack([lax.dynamic_index_in_dim(blocks, p, 0, keepdims=False) for p in picks])


def shards(quantized, scales, d_hidden, w_gate, w_up):
    count, width = quantized.shape
    ff = w_gate.shape[1]
    rows = w_gate.shape[0]
    local = (quantized.astype(F32) * scales).astype(BF16)
    with jax.named_scope("d_hidden_half"):
        far_hidden = swap_half(d_hidden)
    with jax.named_scope("gather_inputs"):
        held = spread(swap_shard_y(local), "zl")
        held, far_hidden = lax.optimization_barrier((held, far_hidden))
        grad_out = jnp.stack([d_hidden, far_hidden]).astype(F32)
        held = held.transpose(1, 0, 2).reshape(count, rows)
        held = spread(held, "y")
        inputs = relative(held)
    with jax.named_scope("all_inputs"):
        all_inputs = lax.all_gather(inputs, "x", axis=0)
    with jax.named_scope("partial_gate_up"):
        w = jnp.concatenate([w_gate, w_up], axis=1)
        parts = jnp.dot(inputs.reshape(4 * count, rows), w, preferred_element_type=F32)
        parts = parts.reshape(2, 2, count, 2 * ff)
    with jax.named_scope("core_sum"):
        parts = parts[0] + swap_core(parts[1].astype(BF16)).astype(F32)
    with jax.named_scope("half_sum"):
        other = swap_half(parts.astype(BF16)).astype(F32)
        pre = parts + other[::-1]
    with jax.named_scope("elementwise"):
        gate, up = pre[..., :ff], pre[..., ff:]
        sig = jax.nn.sigmoid(gate)
        d_gate = (grad_out * up * sig * (1.0 + gate * (1.0 - sig))).astype(BF16)
        d_up = (grad_out * gate * sig).astype(BF16)
        d = jnp.concatenate([d_gate, d_up], axis=-1)
    with jax.named_scope("d_over_x"):
        d_sent, all_inputs = lax.optimization_barrier((d, all_inputs))
        d_all = lax.all_gather(d_sent, "x", axis=0)
    with jax.named_scope("d_core"):
        d_own = jnp.stack([d, swap_core(d)])
    with jax.named_scope("d_input"):
        di = lax.dot_general(
            d_own.reshape(4 * count, 2 * ff), w, (((1,), (1,)), ((), ())), preferred_element_type=F32
        ).astype(BF16)
        di = absolute(di.reshape(4, count, rows))
        di = jnp.sum(lax.all_to_all(di, "y", 0, 0).astype(F32), axis=0).astype(BF16)
        di_y = di
        di = di.reshape(count, 8, width).transpose(1, 0, 2)
        di = jnp.sum(lax.all_to_all(di, "zl", 0, 0).astype(F32), axis=0).astype(BF16)
        di = swap_shard_y(di)
    with jax.named_scope("weight_grads"):
        d_all, _ = lax.optimization_barrier((d_all, di_y))
        d_far = swap_core(d_all)
        mine = all_inputs[:, :2].reshape(8 * count, rows)
        theirs = all_inputs[:, 2:].reshape(8 * count, rows)
        d_all = d_all.reshape(8 * count, 2 * ff)
        d_far = d_far.reshape(8 * count, 2 * ff)
        grads = [
            (
                jnp.dot(mine.T, d_all[:, k : k + ff], preferred_element_type=F32)
                + jnp.dot(theirs.T, d_far[:, k : k + ff], preferred_element_type=F32)
            ).astype(BF16)
            for k in (0, ff)
        ]
    return di, grads[0], grads[1]


def solution(mesh):
    fine = Mesh(mesh.devices.reshape([SIZES[a] for a in AXES]), AXES)
    in_specs = (P(ROWS, COLS), P(ROWS, COLS), P(ROWS, COLS), P(SHARD, COLS), P(SHARD, COLS))
    out_specs = (P(ROWS, COLS), P(SHARD, COLS), P(SHARD, COLS))
    return jax.shard_map(shards, mesh=fine, in_specs=in_specs, out_specs=out_specs, check_vma=False)
```

```python
import jax
import jax.numpy as jnp
import numpy as np
from jax import lax
from jax.experimental import pallas as pl
from jax.experimental.pallas import tpu as pltpu
from jax.sharding import Mesh, PartitionSpec as P

AXES = ("x", "zh", "c", "y", "zl")
SIZES = {"x": 4, "zh": 2, "c": 2, "y": 4, "zl": 8}
ROWS = ("x", "zh", "c")
COLS = ("y", "zl")
SHARD = ("zh", "c")
F32 = jnp.float32
BF16 = jnp.bfloat16


def permute(value, axes, target):
    sizes = [SIZES[a] for a in axes]
    pairs = []
    for i in range(int(np.prod(sizes))):
        at = dict(zip(axes, map(int, np.unravel_index(i, sizes))))
        to = target(at)
        pairs.append((i, int(np.ravel_multi_index([to[a] for a in axes], sizes))))
    return lax.ppermute(value, axes if len(axes) > 1 else axes[0], pairs)


def swap_half_y(value):
    return permute(
        value, ("zh", "y"), lambda d: {"zh": d["y"] // 2, "y": d["zh"] * 2 + d["y"] % 2}
    )


def swap_core(value):
    return permute(value, ("c",), lambda d: {"c": 1 - d["c"]})


def swap_half(value):
    return permute(value, ("zh",), lambda d: {"zh": 1 - d["zh"]})


def step_outer(value, k):
    return permute(value, ("x",), lambda d: {"x": (d["x"] + k) % 4})


def spread(value, axis):
    n = SIZES[axis]
    return lax.all_to_all(jnp.broadcast_to(value[None], (n,) + value.shape), axis, 0, 0)


VMEM = pl.BlockSpec(memory_space=pltpu.VMEM)
SMEM = pl.BlockSpec(memory_space=pltpu.SMEM)
PARAMS = pltpu.CompilerParams(vmem_limit_bytes=32 * 1024 * 1024)


def partial_kernel(core_ref, x_ref, g0_ref, u0_ref, g1_ref, u1_ref, full_ref, send_ref):
    core = core_ref[0]
    ff = g0_ref.shape[1]
    for a in range(2):
        near, far = x_ref[2 * a + core], x_ref[2 * a + 1 - core]
        for k, (w0, w1) in enumerate(((g0_ref, g1_ref), (u0_ref, u1_ref))):
            total = jnp.dot(near, w0[...], preferred_element_type=F32)
            total = total + jnp.dot(far, w1[...], preferred_element_type=F32)
            full_ref[a, :, k * ff : (k + 1) * ff] = total
            send_ref[a, :, k * ff : (k + 1) * ff] = total.astype(BF16)


def partial_gate_up(core, x, weights):
    count, ff = x.shape[1], weights[0].shape[1]
    flops = 2 * 4 * count * x.shape[2] * 2 * ff
    return pl.pallas_call(
        partial_kernel,
        out_shape=(
            jax.ShapeDtypeStruct((2, count, 2 * ff), F32),
            jax.ShapeDtypeStruct((2, count, 2 * ff), BF16),
        ),
        in_specs=[SMEM] + [VMEM] * 5,
        out_specs=(VMEM, VMEM),
        compiler_params=PARAMS,
        cost_estimate=pl.CostEstimate(flops=flops, bytes_accessed=7 << 20, transcendentals=0),
        name="partial_gate_up",
    )(core, x, *weights)


def input_grad_kernel(core_ref, g_ref, u_ref, g0_ref, u0_ref, g1_ref, u1_ref, out_ref):
    core = core_ref[0]
    dims = (((1,), (1,)), ((), ()))
    for w_gate, w_up, b in ((g0_ref, u0_ref, core), (g1_ref, u1_ref, 1 - core)):
        for a in range(2):
            total = lax.dot_general(g_ref[a], w_gate[...], dims, preferred_element_type=F32)
            total = total + lax.dot_general(u_ref[a], w_up[...], dims, preferred_element_type=F32)
            out_ref[2 * a + b] = total.astype(BF16)


def input_grad(core, d_gate, d_up, weights):
    count, rows = d_gate.shape[1], weights[0].shape[0]
    flops = 2 * 4 * count * rows * 2 * d_gate.shape[2]
    return pl.pallas_call(
        input_grad_kernel,
        out_shape=jax.ShapeDtypeStruct((4, count, rows), BF16),
        in_specs=[SMEM] + [VMEM] * 6,
        out_specs=VMEM,
        compiler_params=PARAMS,
        cost_estimate=pl.CostEstimate(flops=flops, bytes_accessed=6 << 20, transcendentals=0),
        name="input_grad",
    )(core, d_gate, d_up, *weights)


def shards(quantized, scales, d_hidden, w_gate, w_up):
    count, width = quantized.shape
    rows, ff = w_gate.shape
    half, core = lax.axis_index("zh"), lax.axis_index("c")
    core_ref = core.astype(jnp.int32).reshape(1)
    with jax.named_scope("weights_of_chip"):
        weights = (w_gate, w_up, swap_core(w_gate), swap_core(w_up))
    local = (quantized.astype(F32) * scales).astype(BF16)
    with jax.named_scope("gather_inputs"):
        held = spread(swap_half_y(local), "zl")
        held = held.transpose(1, 0, 2).reshape(count, rows)
        inputs = spread(held, "y")
    with jax.named_scope("partial_gate_up"):
        parts, sent = partial_gate_up(core_ref, inputs, weights)
    with jax.named_scope("half_sum"):
        inputs, sent = lax.optimization_barrier((inputs, sent))
        other = swap_half(sent)
        far_hidden = swap_half(d_hidden)
    with jax.named_scope("all_inputs"):
        all_inputs = [inputs] + [step_outer(inputs, k) for k in (1, 2, 3)]
    with jax.named_scope("elementwise"):
        pre = parts + other.astype(F32)
        first = half == 0
        grad_out = jnp.stack(
            [jnp.where(first, d_hidden, far_hidden), jnp.where(first, far_hidden, d_hidden)]
        ).astype(F32)
        gate, up = pre[..., :ff], pre[..., ff:]
        sig = jax.nn.sigmoid(gate)
        d_gate = (grad_out * up * sig * (1.0 + gate * (1.0 - sig))).astype(BF16)
        d_up = (grad_out * gate * sig).astype(BF16)
    with jax.named_scope("d_input"):
        di = input_grad(core_ref, d_gate, d_up, weights)
        di_y = jnp.sum(lax.all_to_all(di, "y", 0, 0).astype(F32), axis=0).astype(BF16)
        di = di_y.reshape(count, 8, width).transpose(1, 0, 2)
        di_z = jnp.sum(lax.all_to_all(di, "zl", 0, 0).astype(F32), axis=0).astype(BF16)
        di = swap_half_y(di_z)
    with jax.named_scope("d_over_x"):
        d = jnp.concatenate([d_gate, d_up], axis=-1)
        d_all = lax.all_gather(d, "x", axis=0)
        d_all, all_inputs, _ = lax.optimization_barrier((d_all, all_inputs, di_z))
        outer = lax.axis_index("x")
        d_all = jnp.concatenate(
            [lax.dynamic_index_in_dim(d_all, (outer + 4 - k) % 4, 0, keepdims=False) for k in range(4)]
        ).reshape(8 * count, 2 * ff)
    with jax.named_scope("weight_grads"):

        def grad(b):
            picked = jnp.concatenate(
                [
                    lax.dynamic_index_in_dim(v.reshape(2, 2, count, rows), b, 1, keepdims=False)
                    for v in all_inputs
                ]
            )
            return jnp.dot(picked.reshape(8 * count, rows).T, d_all, preferred_element_type=F32)

        got = swap_core(grad(1 - core).astype(BF16))
        dw = grad(core) + got.astype(F32)
        dw = dw.astype(BF16)
    return di, dw[:, :ff], dw[:, ff:]


def solution(mesh):
    fine = Mesh(mesh.devices.reshape([SIZES[a] for a in AXES]), AXES)
    in_specs = (P(ROWS, COLS), P(ROWS, COLS), P(ROWS, COLS), P(SHARD, COLS), P(SHARD, COLS))
    out_specs = (P(ROWS, COLS), P(SHARD, COLS), P(SHARD, COLS))
    return jax.shard_map(shards, mesh=fine, in_specs=in_specs, out_specs=out_specs, check_vma=False)
```

```python
import jax
import jax.numpy as jnp
import numpy as np
from jax import lax
from jax.experimental import pallas as pl
from jax.experimental.pallas import tpu as pltpu
from jax.sharding import Mesh, PartitionSpec as P

AXES = ("x", "zh", "c", "y", "zl")
SIZES = {"x": 4, "zh": 2, "c": 2, "y": 4, "zl": 8}
ROWS = ("x", "zh", "c")
COLS = ("y", "zl")
SHARD = ("zh", "c")
F32 = jnp.float32
BF16 = jnp.bfloat16


def permute(value, axes, target):
    sizes = [SIZES[a] for a in axes]
    pairs = []
    for i in range(int(np.prod(sizes))):
        at = dict(zip(axes, map(int, np.unravel_index(i, sizes))))
        to = target(at)
        pairs.append((i, int(np.ravel_multi_index([to[a] for a in axes], sizes))))
    return lax.ppermute(value, axes if len(axes) > 1 else axes[0], pairs)


def swap_half_y(value):
    return permute(
        value, ("zh", "y"), lambda d: {"zh": d["y"] // 2, "y": d["zh"] * 2 + d["y"] % 2}
    )


def swap_core(value):
    return permute(value, ("c",), lambda d: {"c": 1 - d["c"]})


def swap_half(value):
    return permute(value, ("zh",), lambda d: {"zh": 1 - d["zh"]})


def step_outer(value, k):
    return permute(value, ("x",), lambda d: {"x": (d["x"] + k) % 4})


def spread(value, axis):
    n = SIZES[axis]
    return lax.all_to_all(jnp.broadcast_to(value[None], (n,) + value.shape), axis, 0, 0)


VMEM = pl.BlockSpec(memory_space=pltpu.VMEM)
SMEM = pl.BlockSpec(memory_space=pltpu.SMEM)
PARAMS = pltpu.CompilerParams(vmem_limit_bytes=32 * 1024 * 1024)


def partial_kernel(place_ref, x_ref, g0_ref, u0_ref, g1_ref, u1_ref, keep_ref, send_ref):
    half, core = place_ref[0], place_ref[1]
    count, ff = x_ref.shape[1], g0_ref.shape[1]

    def rows_of(b):
        return jnp.concatenate([x_ref[2 * (1 - half) + b], x_ref[2 * half + b]], axis=0)

    near, far = rows_of(core), rows_of(1 - core)
    for k, (w0, w1) in enumerate(((g0_ref, g1_ref), (u0_ref, u1_ref))):
        total = jnp.dot(near, w0[...], preferred_element_type=F32)
        total = total + jnp.dot(far, w1[...], preferred_element_type=F32)
        send_ref[:, k * ff : (k + 1) * ff] = total[:count].astype(BF16)
        keep_ref[:, k * ff : (k + 1) * ff] = total[count:]


def partial_gate_up(place, x, weights):
    count, ff = x.shape[1], weights[0].shape[1]
    flops = 2 * 4 * count * x.shape[2] * 2 * ff
    return pl.pallas_call(
        partial_kernel,
        out_shape=(
            jax.ShapeDtypeStruct((count, 2 * ff), F32),
            jax.ShapeDtypeStruct((count, 2 * ff), BF16),
        ),
        in_specs=[SMEM] + [VMEM] * 5,
        out_specs=(VMEM, VMEM),
        compiler_params=PARAMS,
        cost_estimate=pl.CostEstimate(flops=flops, bytes_accessed=6 << 20, transcendentals=0),
        name="partial_gate_up",
    )(place, x, *weights)


def hidden_grad_kernel(keep_ref, other_ref, grad_ref, out_ref):
    ff = grad_ref.shape[1]
    gate = keep_ref[:, :ff] + other_ref[:, :ff].astype(F32)
    up = keep_ref[:, ff:] + other_ref[:, ff:].astype(F32)
    grad_out = grad_ref[...].astype(F32)
    sig = jax.nn.sigmoid(gate)
    out_ref[:, :ff] = (grad_out * up * sig * (1.0 + gate * (1.0 - sig))).astype(BF16)
    out_ref[:, ff:] = (grad_out * gate * sig).astype(BF16)


def hidden_grad(keep, other, grad):
    return pl.pallas_call(
        hidden_grad_kernel,
        out_shape=jax.ShapeDtypeStruct(keep.shape, BF16),
        in_specs=[VMEM] * 3,
        out_specs=VMEM,
        compiler_params=PARAMS,
        cost_estimate=pl.CostEstimate(flops=1 << 20, bytes_accessed=1 << 20, transcendentals=1 << 16),
        name="hidden_grad",
    )(keep, other, grad)


def input_grad_kernel(place_ref, d0_ref, d1_ref, g0_ref, u0_ref, g1_ref, u1_ref, out_ref):
    half, core = place_ref[0], place_ref[1]
    count, ff = d0_ref.shape[0], g0_ref.shape[1]
    dims = (((1,), (1,)), ((), ()))
    d = jnp.concatenate([d0_ref[...], d1_ref[...]], axis=0)
    for w_gate, w_up, b in ((g0_ref, u0_ref, core), (g1_ref, u1_ref, 1 - core)):
        total = lax.dot_general(d[:, :ff], w_gate[...], dims, preferred_element_type=F32)
        total = total + lax.dot_general(d[:, ff:], w_up[...], dims, preferred_element_type=F32)
        out_ref[2 * half + b] = total[:count].astype(BF16)
        out_ref[2 * (1 - half) + b] = total[count:].astype(BF16)


def input_grad(place, d_own, d_other, weights):
    count, rows = d_own.shape[0], weights[0].shape[0]
    flops = 2 * 4 * count * rows * d_own.shape[1]
    return pl.pallas_call(
        input_grad_kernel,
        out_shape=jax.ShapeDtypeStruct((4, count, rows), BF16),
        in_specs=[SMEM] + [VMEM] * 6,
        out_specs=VMEM,
        compiler_params=PARAMS,
        cost_estimate=pl.CostEstimate(flops=flops, bytes_accessed=6 << 20, transcendentals=0),
        name="input_grad",
    )(place, d_own, d_other, *weights)


def weight_grad_kernel(other, place_ref, x_ref, d_ref, out_ref):
    half, core = place_ref[0], place_ref[1]
    b = 1 - core if other else core
    rows = x_ref.shape[2]
    step = 256
    d = jnp.concatenate([d_ref[k] for k in range(8)], axis=0)
    for i in range(0, rows, step):
        x = [x_ref[4 * k + 2 * a + b, :, i : i + step] for k in range(4) for a in (half, 1 - half)]
        total = lax.dot_general(
            jnp.concatenate(x, axis=0), d, (((0,), (0,)), ((), ())), preferred_element_type=F32
        )
        out_ref[i : i + step, :] = total.astype(out_ref.dtype)


def weight_grad(other, place, inputs, d, dtype):
    rows, cols = inputs.shape[2], d.shape[2]
    flops = 2 * 8 * d.shape[1] * rows * cols
    return pl.pallas_call(
        lambda *refs: weight_grad_kernel(other, *refs),
        out_shape=jax.ShapeDtypeStruct((rows, cols), dtype),
        in_specs=[SMEM] + [VMEM] * 2,
        out_specs=VMEM,
        compiler_params=PARAMS,
        cost_estimate=pl.CostEstimate(flops=flops, bytes_accessed=8 << 20, transcendentals=0),
        name="weight_grad_other" if other else "weight_grad_own",
    )(place, inputs, d)


def shards(quantized, scales, d_hidden, w_gate, w_up):
    count, width = quantized.shape
    rows, ff = w_gate.shape
    place = jnp.stack([lax.axis_index("zh"), lax.axis_index("c"), lax.axis_index("x")]).astype(jnp.int32)
    with jax.named_scope("weights_of_chip"):
        weights = (w_gate, w_up, swap_core(w_gate), swap_core(w_up))
    local = (quantized.astype(F32) * scales).astype(BF16)
    with jax.named_scope("gather_inputs"):
        held = spread(swap_half_y(local), "zl")
        held, weights = lax.optimization_barrier((held, weights))
        held = held.transpose(1, 0, 2).reshape(count, rows)
        inputs = spread(held, "y")
    with jax.named_scope("partial_gate_up"):
        keep, sent = partial_gate_up(place, inputs, weights)
    with jax.named_scope("all_inputs"):
        all_inputs = lax.all_gather(inputs, "x", axis=0, tiled=True)
    with jax.named_scope("half_sum"):
        other = swap_half(sent)
    with jax.named_scope("hidden_grad"):
        d_own = hidden_grad(keep, other, d_hidden)
    with jax.named_scope("d_far"):
        d_far = swap_half(d_own)
    with jax.named_scope("d_over_x"):
        d, all_inputs = lax.optimization_barrier((jnp.stack([d_own, d_far]), all_inputs))
        d_all = lax.all_gather(d, "x", axis=0, tiled=True)
    with jax.named_scope("d_input"):
        di = input_grad(place, d_own, d_far, weights)
        di = jnp.sum(lax.all_to_all(di, "y", 0, 0).astype(F32), axis=0).astype(BF16)
        di = di.reshape(count, 8, width).transpose(1, 0, 2)
        di_z = jnp.sum(lax.all_to_all(di, "zl", 0, 0).astype(F32), axis=0).astype(BF16)
        di = swap_half_y(di_z)
    with jax.named_scope("weight_grads"):
        d_all, all_inputs, _ = lax.optimization_barrier((d_all, all_inputs, di_z))
        got = swap_core(weight_grad(True, place, all_inputs, d_all, BF16))
        dw = weight_grad(False, place, all_inputs, d_all, F32)
        d_gate_weight, d_up_weight = (
            (dw[:, k : k + ff] + got[:, k : k + ff].astype(F32)).astype(BF16) for k in (0, ff)
        )
    return di, d_gate_weight, d_up_weight


def solution(mesh):
    fine = Mesh(mesh.devices.reshape([SIZES[a] for a in AXES]), AXES)
    in_specs = (P(ROWS, COLS), P(ROWS, COLS), P(ROWS, COLS), P(SHARD, COLS), P(SHARD, COLS))
    out_specs = (P(ROWS, COLS), P(SHARD, COLS), P(SHARD, COLS))
    return jax.shard_map(shards, mesh=fine, in_specs=in_specs, out_specs=out_specs, check_vma=False)
```

```python
import jax
import jax.numpy as jnp
import numpy as np
from jax import lax
from jax.experimental import pallas as pl
from jax.experimental.pallas import tpu as pltpu
from jax.sharding import Mesh, PartitionSpec as P

AXES = ("x", "zh", "c", "y", "zl")
SIZES = {"x": 4, "zh": 2, "c": 2, "y": 4, "zl": 8}
ROWS = ("x", "zh", "c")
COLS = ("y", "zl")
SHARD = ("zh", "c")
F32 = jnp.float32
BF16 = jnp.bfloat16


def permute(value, axes, target):
    sizes = [SIZES[a] for a in axes]
    pairs = []
    for i in range(int(np.prod(sizes))):
        at = dict(zip(axes, map(int, np.unravel_index(i, sizes))))
        to = target(at)
        pairs.append((i, int(np.ravel_multi_index([to[a] for a in axes], sizes))))
    return lax.ppermute(value, axes if len(axes) > 1 else axes[0], pairs)


def swap_half_y(value):
    return permute(
        value, ("zh", "y"), lambda d: {"zh": d["y"] // 2, "y": d["zh"] * 2 + d["y"] % 2}
    )


def swap_core(value):
    return permute(value, ("c",), lambda d: {"c": 1 - d["c"]})


def swap_half(value):
    return permute(value, ("zh",), lambda d: {"zh": 1 - d["zh"]})


def step_outer(value, k):
    return permute(value, ("x",), lambda d: {"x": (d["x"] + k) % 4})


def spread(value, axis):
    n = SIZES[axis]
    return lax.all_to_all(jnp.broadcast_to(value[None], (n,) + value.shape), axis, 0, 0)


VMEM = pl.BlockSpec(memory_space=pltpu.VMEM)
HBM = pl.BlockSpec(memory_space=pltpu.MemorySpace.HBM)
SMEM = pl.BlockSpec(memory_space=pltpu.SMEM)
PARAMS = pltpu.CompilerParams(vmem_limit_bytes=24 * 1024 * 1024)


def partial_kernel(place_ref, x_ref, g_ref, u_ref, keep_ref, send_ref):
    half = place_ref[0]
    count, ff = x_ref.shape[1], g_ref.shape[2]
    x = [jnp.concatenate([x_ref[2 * (1 - half) + b], x_ref[2 * half + b]], axis=0) for b in range(2)]
    for k, w in enumerate((g_ref, u_ref)):
        total = jnp.dot(x[0], w[0], preferred_element_type=F32)
        total = total + jnp.dot(x[1], w[1], preferred_element_type=F32)
        send_ref[:, k * ff : (k + 1) * ff] = total[:count].astype(BF16)
        keep_ref[:, k * ff : (k + 1) * ff] = total[count:]


def partial_gate_up(place, x, weights):
    count, ff = x.shape[1], weights[0].shape[2]
    flops = 2 * 4 * count * x.shape[2] * 2 * ff
    return pl.pallas_call(
        partial_kernel,
        out_shape=(
            jax.ShapeDtypeStruct((count, 2 * ff), F32),
            jax.ShapeDtypeStruct((count, 2 * ff), BF16),
        ),
        in_specs=[SMEM] + [VMEM] * 3,
        out_specs=(VMEM, VMEM),
        compiler_params=PARAMS,
        cost_estimate=pl.CostEstimate(flops=flops, bytes_accessed=6 << 20, transcendentals=0),
        name="partial_gate_up",
    )(place, x, *weights)


def hidden_grad_kernel(keep_ref, other_ref, grad_ref, out_ref):
    ff = grad_ref.shape[1]
    gate = keep_ref[:, :ff] + other_ref[:, :ff].astype(F32)
    up = keep_ref[:, ff:] + other_ref[:, ff:].astype(F32)
    grad_out = grad_ref[...].astype(F32)
    sig = jax.nn.sigmoid(gate)
    out_ref[:, :ff] = (grad_out * up * sig * (1.0 + gate * (1.0 - sig))).astype(BF16)
    out_ref[:, ff:] = (grad_out * gate * sig).astype(BF16)


def hidden_grad(keep, other, grad):
    return pl.pallas_call(
        hidden_grad_kernel,
        out_shape=jax.ShapeDtypeStruct(keep.shape, BF16),
        in_specs=[VMEM] * 3,
        out_specs=VMEM,
        compiler_params=PARAMS,
        cost_estimate=pl.CostEstimate(flops=1 << 20, bytes_accessed=1 << 20, transcendentals=1 << 16),
        name="hidden_grad",
    )(keep, other, grad)


def input_grad_kernel(place_ref, d0_ref, d1_ref, g_ref, u_ref, out_ref, both_ref):
    half = place_ref[0]
    count, ff = d0_ref.shape[0], g_ref.shape[2]
    dims = (((1,), (1,)), ((), ()))
    both_ref[0], both_ref[1] = d0_ref[...], d1_ref[...]
    d = jnp.concatenate([d0_ref[...], d1_ref[...]], axis=0)
    for b in range(2):
        total = lax.dot_general(d[:, :ff], g_ref[b], dims, preferred_element_type=F32)
        total = total + lax.dot_general(d[:, ff:], u_ref[b], dims, preferred_element_type=F32)
        out_ref[2 * half + b] = total[:count].astype(BF16)
        out_ref[2 * (1 - half) + b] = total[count:].astype(BF16)


def input_grad(place, d_own, d_other, weights):
    (count, cols), rows = d_own.shape, weights[0].shape[1]
    flops = 2 * 4 * count * rows * cols
    return pl.pallas_call(
        input_grad_kernel,
        out_shape=(
            jax.ShapeDtypeStruct((4, count, rows), BF16),
            jax.ShapeDtypeStruct((2, count, cols), BF16),
        ),
        in_specs=[SMEM] + [VMEM] * 4,
        out_specs=(VMEM, VMEM),
        compiler_params=PARAMS,
        cost_estimate=pl.CostEstimate(flops=flops, bytes_accessed=6 << 20, transcendentals=0),
        name="input_grad",
    )(place, d_own, d_other, *weights)


STEP = 256


def weight_grad_rows(place_ref, x_ref, d_ref, x_held, d_held, x_sem, d_sem, other):
    half, core = place_ref[0], place_ref[1]
    b = 1 - core if other else core
    tiles = x_ref.shape[3] // STEP

    def columns(i):
        return pltpu.make_async_copy(
            x_ref.at[:, b, :, pl.ds(i * STEP, STEP)], x_held.at[i], x_sem.at[i]
        )

    def tokens(a):
        r = half if a == 0 else 1 - half
        return pltpu.make_async_copy(d_ref.at[:, r], d_held.at[:, a], d_sem.at[a])

    copies = [tokens(0), tokens(1)] + [columns(i) for i in range(tiles)]
    for copy in copies:
        copy.start()
    copies[0].wait()
    copies[1].wait()
    d = d_held[...].reshape(-1, d_held.shape[3])
    for i in range(tiles):
        copies[2 + i].wait()
        x = x_held[i].reshape(-1, STEP)
        yield slice(i * STEP, (i + 1) * STEP), lax.dot_general(
            x, d, (((0,), (0,)), ((), ())), preferred_element_type=F32
        )


def weight_grad_other_kernel(place_ref, x_ref, d_ref, out_ref, *scratch):
    for at, total in weight_grad_rows(place_ref, x_ref, d_ref, *scratch, True):
        out_ref[at, :] = total.astype(BF16)


def weight_grad_own_kernel(place_ref, x_ref, d_ref, got_ref, gate_ref, up_ref, *scratch):
    ff = gate_ref.shape[1]
    *scratch, got_held, got_sem = scratch
    copy = pltpu.make_async_copy(got_ref, got_held, got_sem.at[0])
    copy.start()
    for at, total in weight_grad_rows(place_ref, x_ref, d_ref, *scratch, False):
        if at.start == 0:
            copy.wait()
        total = (total + got_held[at, :].astype(F32)).astype(BF16)
        gate_ref[at, :] = total[:, :ff]
        up_ref[at, :] = total[:, ff:]


def weight_grad(kernel, name, place, inputs, d, got, shapes):
    pairs, _, count, rows = inputs.shape
    cols = d.shape[3]
    flops = 2 * pairs * count * rows * cols
    return pl.pallas_call(
        kernel,
        out_shape=[jax.ShapeDtypeStruct(v, BF16) for v in shapes],
        in_specs=[SMEM, HBM, HBM] + [HBM] * len(got),
        out_specs=[VMEM] * len(shapes),
        scratch_shapes=[
            pltpu.VMEM((rows // STEP, pairs, count, STEP), BF16),
            pltpu.VMEM((pairs // 2, 2, count, cols), BF16),
            pltpu.SemaphoreType.DMA((rows // STEP,)),
            pltpu.SemaphoreType.DMA((2,)),
        ]
        + [v for g in got for v in (pltpu.VMEM(g.shape, BF16), pltpu.SemaphoreType.DMA((1,)))],
        compiler_params=pltpu.CompilerParams(vmem_limit_bytes=58 * 1024 * 1024),
        cost_estimate=pl.CostEstimate(flops=flops, bytes_accessed=8 << 20, transcendentals=0),
        name=name,
    )(place, inputs, d, *got)


def shards(quantized, scales, d_hidden, w_gate, w_up):
    count, width = quantized.shape
    rows, ff = w_gate.shape
    place = jnp.stack([lax.axis_index("zh"), lax.axis_index("c"), lax.axis_index("x")]).astype(jnp.int32)
    with jax.named_scope("weights_of_chip"):
        weights = tuple(lax.all_gather(w, "c", axis=0) for w in (w_gate, w_up))
    local = (quantized.astype(F32) * scales).astype(BF16)
    with jax.named_scope("gather_inputs"):
        held = spread(swap_half_y(local), "zl")
        held, weights = lax.optimization_barrier((held, weights))
        held = held.transpose(1, 0, 2).reshape(count, rows)
        inputs = spread(held, "y")
    with jax.named_scope("partial_gate_up"):
        keep, sent = partial_gate_up(place, inputs, weights)
    with jax.named_scope("all_inputs"):
        all_inputs = lax.all_gather(inputs, "x", axis=0, tiled=True)
    with jax.named_scope("half_sum"):
        other = swap_half(sent)
    with jax.named_scope("hidden_grad"):
        d_own = hidden_grad(keep, other, d_hidden)
    with jax.named_scope("d_far"):
        d_far = swap_half(d_own)
    with jax.named_scope("d_input"):
        di, d_both = input_grad(place, d_own, d_far, weights)
        di = jnp.sum(lax.all_to_all(di, "y", 0, 0).astype(F32), axis=0).astype(BF16)
        di = di.reshape(count, 8, width).transpose(1, 0, 2)
        di_z = jnp.sum(lax.all_to_all(di, "zl", 0, 0).astype(F32), axis=0).astype(BF16)
        di = swap_half_y(di_z)
    with jax.named_scope("d_over_x"):
        d_both, all_inputs = lax.optimization_barrier((d_both, all_inputs))
        d_all = lax.all_gather(d_both, "x", axis=0, tiled=True)
    with jax.named_scope("weight_grads"):
        d_all, _ = lax.optimization_barrier((d_all, di_z))
        d_all = d_all.reshape(4, 2, count, 2 * ff)
        all_inputs = all_inputs.reshape(8, 2, count, rows)
        (sent,) = weight_grad(
            weight_grad_other_kernel, "weight_grad_other", place, all_inputs, d_all, (), [(rows, 2 * ff)]
        )
        d_gate_weight, d_up_weight = weight_grad(
            weight_grad_own_kernel,
            "weight_grad_own",
            place,
            all_inputs,
            d_all,
            (swap_core(sent),),
            [(rows, ff)] * 2,
        )
    return lax.optimization_barrier((di, d_gate_weight, d_up_weight))


def solution(mesh):
    fine = Mesh(mesh.devices.reshape([SIZES[a] for a in AXES]), AXES)
    in_specs = (P(ROWS, COLS), P(ROWS, COLS), P(ROWS, COLS), P(SHARD, COLS), P(SHARD, COLS))
    out_specs = (P(ROWS, COLS), P(SHARD, COLS), P(SHARD, COLS))
    return jax.shard_map(shards, mesh=fine, in_specs=in_specs, out_specs=out_specs, check_vma=False)
```

```python
import jax
import jax.numpy as jnp
import numpy as np
from jax import lax
from jax.experimental import pallas as pl
from jax.experimental.pallas import tpu as pltpu
from jax.sharding import Mesh, PartitionSpec as P

AXES = ("x", "zh", "c", "y", "zl")
SIZES = {"x": 4, "zh": 2, "c": 2, "y": 4, "zl": 8}
ROWS = ("x", "zh", "c")
COLS = ("y", "zl")
SHARD = ("zh", "c")
F32 = jnp.float32
BF16 = jnp.bfloat16


def permute(value, axes, target):
    sizes = [SIZES[a] for a in axes]
    pairs = []
    for i in range(int(np.prod(sizes))):
        at = dict(zip(axes, map(int, np.unravel_index(i, sizes))))
        to = target(at)
        pairs.append((i, int(np.ravel_multi_index([to[a] for a in axes], sizes))))
    return lax.ppermute(value, axes if len(axes) > 1 else axes[0], pairs)


def swap_half_y(value):
    return permute(
        value, ("zh", "y"), lambda d: {"zh": d["y"] // 2, "y": d["zh"] * 2 + d["y"] % 2}
    )


def swap_core(value):
    return permute(value, ("c",), lambda d: {"c": 1 - d["c"]})


def swap_half(value):
    return permute(value, ("zh",), lambda d: {"zh": 1 - d["zh"]})


def step_outer(value, k):
    return permute(value, ("x",), lambda d: {"x": (d["x"] + k) % 4})


def spread(value, axis):
    n = SIZES[axis]
    return lax.all_to_all(jnp.broadcast_to(value[None], (n,) + value.shape), axis, 0, 0)


VMEM = pl.BlockSpec(memory_space=pltpu.VMEM)
SMEM = pl.BlockSpec(memory_space=pltpu.SMEM)
PARAMS = pltpu.CompilerParams(vmem_limit_bytes=12 * 1024 * 1024)


def partial_kernel(place_ref, x_ref, g0_ref, u0_ref, g1_ref, u1_ref, keep_ref, send_ref):
    half, core = place_ref[0], place_ref[1]
    count, ff = x_ref.shape[1], g0_ref.shape[1]

    def rows_of(b):
        return jnp.concatenate([x_ref[2 * (1 - half) + b], x_ref[2 * half + b]], axis=0)

    near, far = rows_of(core), rows_of(1 - core)
    for k, (w0, w1) in enumerate(((g0_ref, g1_ref), (u0_ref, u1_ref))):
        total = jnp.dot(near, w0[...], preferred_element_type=F32)
        total = total + jnp.dot(far, w1[...], preferred_element_type=F32)
        send_ref[:, k * ff : (k + 1) * ff] = total[:count].astype(BF16)
        keep_ref[:, k * ff : (k + 1) * ff] = total[count:]


def partial_gate_up(place, x, weights):
    count, ff = x.shape[1], weights[0].shape[1]
    flops = 2 * 4 * count * x.shape[2] * 2 * ff
    return pl.pallas_call(
        partial_kernel,
        out_shape=(
            jax.ShapeDtypeStruct((count, 2 * ff), F32),
            jax.ShapeDtypeStruct((count, 2 * ff), BF16),
        ),
        in_specs=[SMEM] + [VMEM] * 5,
        out_specs=(VMEM, VMEM),
        compiler_params=PARAMS,
        cost_estimate=pl.CostEstimate(flops=flops, bytes_accessed=6 << 20, transcendentals=0),
        name="partial_gate_up",
    )(place, x, *weights)


def hidden_grad_kernel(keep_ref, other_ref, grad_ref, out_ref):
    ff = grad_ref.shape[1]
    gate = keep_ref[:, :ff] + other_ref[:, :ff].astype(F32)
    up = keep_ref[:, ff:] + other_ref[:, ff:].astype(F32)
    grad_out = grad_ref[...].astype(F32)
    sig = jax.nn.sigmoid(gate)
    out_ref[:, :ff] = (grad_out * up * sig * (1.0 + gate * (1.0 - sig))).astype(BF16)
    out_ref[:, ff:] = (grad_out * gate * sig).astype(BF16)


def hidden_grad(keep, other, grad):
    return pl.pallas_call(
        hidden_grad_kernel,
        out_shape=jax.ShapeDtypeStruct(keep.shape, BF16),
        in_specs=[VMEM] * 3,
        out_specs=VMEM,
        compiler_params=PARAMS,
        cost_estimate=pl.CostEstimate(flops=1 << 20, bytes_accessed=1 << 20, transcendentals=1 << 16),
        name="hidden_grad",
    )(keep, other, grad)


def input_grad_kernel(place_ref, d0_ref, d1_ref, g0_ref, u0_ref, g1_ref, u1_ref, out_ref):
    half, core = place_ref[0], place_ref[1]
    count, ff = d0_ref.shape[0], g0_ref.shape[1]
    dims = (((1,), (1,)), ((), ()))
    d = jnp.concatenate([d0_ref[...], d1_ref[...]], axis=0)
    for w_gate, w_up, b in ((g0_ref, u0_ref, core), (g1_ref, u1_ref, 1 - core)):
        total = lax.dot_general(d[:, :ff], w_gate[...], dims, preferred_element_type=F32)
        total = total + lax.dot_general(d[:, ff:], w_up[...], dims, preferred_element_type=F32)
        out_ref[2 * half + b] = total[:count].astype(BF16)
        out_ref[2 * (1 - half) + b] = total[count:].astype(BF16)


def input_grad(place, d_own, d_other, weights):
    (count, cols), rows = d_own.shape, weights[0].shape[0]
    flops = 2 * 4 * count * rows * cols
    return pl.pallas_call(
        input_grad_kernel,
        out_shape=jax.ShapeDtypeStruct((4, count, rows), BF16),
        in_specs=[SMEM] + [VMEM] * 6,
        out_specs=VMEM,
        compiler_params=PARAMS,
        cost_estimate=pl.CostEstimate(flops=flops, bytes_accessed=6 << 20, transcendentals=0),
        name="input_grad",
    )(place, d_own, d_other, *weights)


def weight_grad_rows(place_ref, x_ref, d_ref, other):
    half, core = place_ref[0], place_ref[1]
    b = 1 - core if other else core
    step = 256
    d = jnp.concatenate([d_ref[k] for k in range(8)], axis=0)
    for i in range(0, x_ref.shape[2], step):
        x = [x_ref[4 * k + 2 * a + b, :, i : i + step] for k in range(4) for a in (half, 1 - half)]
        yield slice(i, i + step), lax.dot_general(
            jnp.concatenate(x, axis=0), d, (((0,), (0,)), ((), ())), preferred_element_type=F32
        )


def weight_grad_other_kernel(place_ref, x_ref, d_ref, out_ref):
    for at, total in weight_grad_rows(place_ref, x_ref, d_ref, True):
        out_ref[at, :] = total.astype(BF16)


def weight_grad_own_kernel(place_ref, x_ref, d_ref, got_ref, gate_ref, up_ref):
    ff = gate_ref.shape[1]
    for at, total in weight_grad_rows(place_ref, x_ref, d_ref, False):
        total = (total + got_ref[at, :].astype(F32)).astype(BF16)
        gate_ref[at, :] = total[:, :ff]
        up_ref[at, :] = total[:, ff:]


def weight_grad(kernel, name, place, inputs, d, got, shapes):
    flops = 2 * 8 * d.shape[1] * inputs.shape[2] * d.shape[2]
    return pl.pallas_call(
        kernel,
        out_shape=[jax.ShapeDtypeStruct(v, BF16) for v in shapes],
        in_specs=[SMEM] + [VMEM] * (2 + len(got)),
        out_specs=[VMEM] * len(shapes),
        compiler_params=PARAMS,
        cost_estimate=pl.CostEstimate(flops=flops, bytes_accessed=8 << 20, transcendentals=0),
        name=name,
    )(place, inputs, d, *got)


def shards(quantized, scales, d_hidden, w_gate, w_up):
    count, width = quantized.shape
    rows, ff = w_gate.shape
    place = jnp.stack([lax.axis_index("zh"), lax.axis_index("c"), lax.axis_index("x")]).astype(jnp.int32)
    local = (quantized.astype(F32) * scales).astype(BF16)
    with jax.named_scope("gather_inputs"):
        held, gate_sent, up_sent = lax.optimization_barrier((swap_half_y(local), w_gate, w_up))
        others = swap_core(gate_sent), swap_core(up_sent)
        held = spread(held, "zl")
        held, *others = lax.optimization_barrier((held, *others))
        weights = (w_gate, w_up, *others)
        held = held.transpose(1, 0, 2).reshape(count, rows)
        inputs = spread(held, "y")
    with jax.named_scope("partial_gate_up"):
        keep, sent = partial_gate_up(place, inputs, weights)
    with jax.named_scope("all_inputs"):
        all_inputs = lax.all_gather(inputs, "x", axis=0, tiled=True)
    with jax.named_scope("half_sum"):
        other = swap_half(sent)
    with jax.named_scope("hidden_grad"):
        d_own = hidden_grad(keep, other, d_hidden)
    with jax.named_scope("d_far"):
        d_far = swap_half(d_own)
    with jax.named_scope("d_input"):
        di = input_grad(place, d_own, d_far, weights)
        di, d_own, d_far = lax.optimization_barrier((di, d_own, d_far))
        di = jnp.sum(lax.all_to_all(di, "y", 0, 0).astype(F32), axis=0).astype(BF16)
        di = di.reshape(count, 8, width).transpose(1, 0, 2)
        di_z = jnp.sum(lax.all_to_all(di, "zl", 0, 0).astype(F32), axis=0).astype(BF16)
        di = swap_half_y(di_z)
    with jax.named_scope("d_over_x"):
        d_both, all_inputs = lax.optimization_barrier((jnp.stack([d_own, d_far]), all_inputs))
        d_all = lax.all_gather(d_both, "x", axis=0, tiled=True)
    with jax.named_scope("weight_grads"):
        d_all, _ = lax.optimization_barrier((d_all, di_z))
        (sent,) = weight_grad(
            weight_grad_other_kernel, "weight_grad_other", place, all_inputs, d_all, (), [(rows, 2 * ff)]
        )
        d_gate_weight, d_up_weight = weight_grad(
            weight_grad_own_kernel,
            "weight_grad_own",
            place,
            all_inputs,
            d_all,
            (swap_core(sent),),
            [(rows, ff)] * 2,
        )
    return lax.optimization_barrier((di, d_gate_weight, d_up_weight))


def solution(mesh):
    fine = Mesh(mesh.devices.reshape([SIZES[a] for a in AXES]), AXES)
    in_specs = (P(ROWS, COLS), P(ROWS, COLS), P(ROWS, COLS), P(SHARD, COLS), P(SHARD, COLS))
    out_specs = (P(ROWS, COLS), P(SHARD, COLS), P(SHARD, COLS))
    return jax.shard_map(shards, mesh=fine, in_specs=in_specs, out_specs=out_specs, check_vma=False)
```

```python
import jax
import jax.numpy as jnp
import numpy as np
from jax import lax
from jax.experimental import pallas as pl
from jax.experimental.pallas import tpu as pltpu
from jax.sharding import Mesh, PartitionSpec as P

AXES = ("x", "zh", "c", "y", "zl")
SIZES = {"x": 4, "zh": 2, "c": 2, "y": 4, "zl": 8}
ROWS = ("x", "zh", "c")
COLS = ("y", "zl")
SHARD = ("zh", "c")
F32 = jnp.float32
BF16 = jnp.bfloat16


def permute(value, axes, target):
    sizes = [SIZES[a] for a in axes]
    pairs = []
    for i in range(int(np.prod(sizes))):
        at = dict(zip(axes, map(int, np.unravel_index(i, sizes))))
        to = target(at)
        pairs.append((i, int(np.ravel_multi_index([to[a] for a in axes], sizes))))
    return lax.ppermute(value, axes if len(axes) > 1 else axes[0], pairs)


def swap_half_y(value):
    return permute(
        value, ("zh", "y"), lambda d: {"zh": d["y"] // 2, "y": d["zh"] * 2 + d["y"] % 2}
    )


def swap_core(value):
    return permute(value, ("c",), lambda d: {"c": 1 - d["c"]})


def swap_half(value):
    return permute(value, ("zh",), lambda d: {"zh": 1 - d["zh"]})


def step_outer(value, k):
    return permute(value, ("x",), lambda d: {"x": (d["x"] + k) % 4})


def spread(value, axis):
    n = SIZES[axis]
    return lax.all_to_all(jnp.broadcast_to(value[None], (n,) + value.shape), axis, 0, 0)


VMEM = pl.BlockSpec(memory_space=pltpu.VMEM)
SMEM = pl.BlockSpec(memory_space=pltpu.SMEM)
PARAMS = pltpu.CompilerParams(vmem_limit_bytes=12 * 1024 * 1024)


def partial_kernel(place_ref, x_ref, g0_ref, u0_ref, g1_ref, u1_ref, keep_ref, send_ref):
    half, core = place_ref[0], place_ref[1]
    count, ff = x_ref.shape[1], g0_ref.shape[1]

    def rows_of(b):
        return jnp.concatenate([x_ref[2 * (1 - half) + b], x_ref[2 * half + b]], axis=0)

    near, far = rows_of(core), rows_of(1 - core)
    for k, (w0, w1) in enumerate(((g0_ref, g1_ref), (u0_ref, u1_ref))):
        total = jnp.dot(near, w0[...], preferred_element_type=F32)
        total = total + jnp.dot(far, w1[...], preferred_element_type=F32)
        send_ref[:, k * ff : (k + 1) * ff] = total[:count].astype(BF16)
        keep_ref[:, k * ff : (k + 1) * ff] = total[count:]


def partial_gate_up(place, x, weights):
    count, ff = x.shape[1], weights[0].shape[1]
    flops = 2 * 4 * count * x.shape[2] * 2 * ff
    return pl.pallas_call(
        partial_kernel,
        out_shape=(
            jax.ShapeDtypeStruct((count, 2 * ff), F32),
            jax.ShapeDtypeStruct((count, 2 * ff), BF16),
        ),
        in_specs=[SMEM] + [VMEM] * 5,
        out_specs=(VMEM, VMEM),
        compiler_params=PARAMS,
        cost_estimate=pl.CostEstimate(flops=flops, bytes_accessed=6 << 20, transcendentals=0),
        name="partial_gate_up",
    )(place, x, *weights)


def hidden_grad_kernel(keep_ref, other_ref, grad_ref, out_ref):
    ff = grad_ref.shape[1]
    gate = keep_ref[:, :ff] + other_ref[:, :ff].astype(F32)
    up = keep_ref[:, ff:] + other_ref[:, ff:].astype(F32)
    grad_out = grad_ref[...].astype(F32)
    sig = jax.nn.sigmoid(gate)
    out_ref[:, :ff] = (grad_out * up * sig * (1.0 + gate * (1.0 - sig))).astype(BF16)
    out_ref[:, ff:] = (grad_out * gate * sig).astype(BF16)


def hidden_grad(keep, other, grad):
    return pl.pallas_call(
        hidden_grad_kernel,
        out_shape=jax.ShapeDtypeStruct(keep.shape, BF16),
        in_specs=[VMEM] * 3,
        out_specs=VMEM,
        compiler_params=PARAMS,
        cost_estimate=pl.CostEstimate(flops=1 << 20, bytes_accessed=1 << 20, transcendentals=1 << 16),
        name="hidden_grad",
    )(keep, other, grad)


def input_grad_kernel(place_ref, d0_ref, d1_ref, g0_ref, u0_ref, g1_ref, u1_ref, out_ref):
    half, core = place_ref[0], place_ref[1]
    count, ff = d0_ref.shape[0], g0_ref.shape[1]
    dims = (((1,), (1,)), ((), ()))
    d = jnp.concatenate([d0_ref[...], d1_ref[...]], axis=0)
    for w_gate, w_up, b in ((g0_ref, u0_ref, core), (g1_ref, u1_ref, 1 - core)):
        total = lax.dot_general(d[:, :ff], w_gate[...], dims, preferred_element_type=F32)
        total = total + lax.dot_general(d[:, ff:], w_up[...], dims, preferred_element_type=F32)
        out_ref[2 * half + b] = total[:count].astype(BF16)
        out_ref[2 * (1 - half) + b] = total[count:].astype(BF16)


def input_grad(place, d_own, d_other, weights):
    (count, cols), rows = d_own.shape, weights[0].shape[0]
    flops = 2 * 4 * count * rows * cols
    return pl.pallas_call(
        input_grad_kernel,
        out_shape=jax.ShapeDtypeStruct((4, count, rows), BF16),
        in_specs=[SMEM] + [VMEM] * 6,
        out_specs=VMEM,
        compiler_params=PARAMS,
        cost_estimate=pl.CostEstimate(flops=flops, bytes_accessed=6 << 20, transcendentals=0),
        name="input_grad",
    )(place, d_own, d_other, *weights)


def weight_grad_rows(place_ref, x_ref, d_ref, other):
    half, core = place_ref[0], place_ref[1]
    b = 1 - core if other else core
    step = 256
    d = jnp.concatenate([d_ref[k] for k in range(8)], axis=0)
    for i in range(0, x_ref.shape[2], step):
        x = [x_ref[4 * k + 2 * a + b, :, i : i + step] for k in range(4) for a in (half, 1 - half)]
        yield slice(i, i + step), lax.dot_general(
            jnp.concatenate(x, axis=0), d, (((0,), (0,)), ((), ())), preferred_element_type=F32
        )


def weight_grad_other_kernel(place_ref, x_ref, d_ref, out_ref):
    for at, total in weight_grad_rows(place_ref, x_ref, d_ref, True):
        out_ref[at, :] = total.astype(BF16)


def weight_grad_own_kernel(place_ref, x_ref, d_ref, got_ref, gate_ref, up_ref):
    ff = gate_ref.shape[1]
    for at, total in weight_grad_rows(place_ref, x_ref, d_ref, False):
        total = (total + got_ref[at, :].astype(F32)).astype(BF16)
        gate_ref[at, :] = total[:, :ff]
        up_ref[at, :] = total[:, ff:]


def weight_grad(kernel, name, place, inputs, d, got, shapes):
    flops = 2 * 8 * d.shape[1] * inputs.shape[2] * d.shape[2]
    return pl.pallas_call(
        kernel,
        out_shape=[jax.ShapeDtypeStruct(v, BF16) for v in shapes],
        in_specs=[SMEM] + [VMEM] * (2 + len(got)),
        out_specs=[VMEM] * len(shapes),
        compiler_params=PARAMS,
        cost_estimate=pl.CostEstimate(flops=flops, bytes_accessed=8 << 20, transcendentals=0),
        name=name,
    )(place, inputs, d, *got)


def shards(quantized, scales, d_hidden, w_gate, w_up):
    count, width = quantized.shape
    rows, ff = w_gate.shape
    place = jnp.stack([lax.axis_index("zh"), lax.axis_index("c"), lax.axis_index("x")]).astype(jnp.int32)
    local = (quantized.astype(F32) * scales).astype(BF16)
    with jax.named_scope("gather_inputs"):
        held = spread(swap_half_y(local), "zl")
        held = held.transpose(1, 0, 2).reshape(count, rows)
        inputs = spread(held, "y")
        inputs, *others = lax.optimization_barrier((inputs, swap_core(w_gate), swap_core(w_up)))
        weights = (w_gate, w_up, *others)
    with jax.named_scope("partial_gate_up"):
        keep, sent = partial_gate_up(place, inputs, weights)
        inputs, sent = lax.optimization_barrier((inputs, sent))
    with jax.named_scope("all_inputs"):
        all_inputs = lax.all_gather(inputs, "x", axis=0, tiled=True)
    with jax.named_scope("half_sum"):
        other = swap_half(sent)
    with jax.named_scope("hidden_grad"):
        d_own = hidden_grad(keep, other, d_hidden)
    with jax.named_scope("d_far"):
        d_far = swap_half(d_own)
    with jax.named_scope("d_input"):
        di = input_grad(place, d_own, d_far, weights)
        di, d_own, d_far = lax.optimization_barrier((di, d_own, d_far))
        di = jnp.sum(lax.all_to_all(di, "y", 0, 0).astype(F32), axis=0).astype(BF16)
        di = di.reshape(count, 8, width).transpose(1, 0, 2)
        di = lax.all_to_all(di, "zl", 0, 0)
    with jax.named_scope("d_over_x"):
        d_both, all_inputs = lax.optimization_barrier((jnp.stack([d_own, d_far]), all_inputs))
        d_all = lax.all_gather(d_both, "x", axis=0, tiled=True)
    with jax.named_scope("weight_grads"):
        (sent,) = weight_grad(
            weight_grad_other_kernel, "weight_grad_other", place, all_inputs, d_all, (), [(rows, 2 * ff)]
        )
        di, sent = lax.optimization_barrier((di, sent))
        d_gate_weight, d_up_weight = weight_grad(
            weight_grad_own_kernel,
            "weight_grad_own",
            place,
            all_inputs,
            d_all,
            (swap_core(sent),),
            [(rows, ff)] * 2,
        )
    with jax.named_scope("d_input"):
        di = swap_half_y(jnp.sum(di.astype(F32), axis=0).astype(BF16))
    return lax.optimization_barrier((di, d_gate_weight, d_up_weight))


def solution(mesh):
    fine = Mesh(mesh.devices.reshape([SIZES[a] for a in AXES]), AXES)
    in_specs = (P(ROWS, COLS), P(ROWS, COLS), P(ROWS, COLS), P(SHARD, COLS), P(SHARD, COLS))
    out_specs = (P(ROWS, COLS), P(SHARD, COLS), P(SHARD, COLS))
    return jax.shard_map(shards, mesh=fine, in_specs=in_specs, out_specs=out_specs, check_vma=False)
```

```python
import jax
import jax.numpy as jnp
import numpy as np
from jax import lax
from jax.experimental import pallas as pl
from jax.experimental.pallas import tpu as pltpu
from jax.sharding import Mesh, PartitionSpec as P

AXES = ("x", "zh", "c", "y", "zl")
SIZES = {"x": 4, "zh": 2, "c": 2, "y": 4, "zl": 8}
ROWS = ("x", "zh", "c")
COLS = ("y", "zl")
SHARD = ("zh", "c")
F32 = jnp.float32
BF16 = jnp.bfloat16


def permute(value, axes, target):
    sizes = [SIZES[a] for a in axes]
    pairs = []
    for i in range(int(np.prod(sizes))):
        at = dict(zip(axes, map(int, np.unravel_index(i, sizes))))
        to = target(at)
        pairs.append((i, int(np.ravel_multi_index([to[a] for a in axes], sizes))))
    return lax.ppermute(value, axes if len(axes) > 1 else axes[0], pairs)


def swap_half_y(value):
    return permute(
        value, ("zh", "y"), lambda d: {"zh": d["y"] // 2, "y": d["zh"] * 2 + d["y"] % 2}
    )


def swap_core(value):
    return permute(value, ("c",), lambda d: {"c": 1 - d["c"]})


def swap_half(value):
    return permute(value, ("zh",), lambda d: {"zh": 1 - d["zh"]})


def step_outer(value, k):
    return permute(value, ("x",), lambda d: {"x": (d["x"] + k) % 4})


def spread(value, axis):
    n = SIZES[axis]
    return lax.all_to_all(jnp.broadcast_to(value[None], (n,) + value.shape), axis, 0, 0)


VMEM = pl.BlockSpec(memory_space=pltpu.VMEM)
HBM = pl.BlockSpec(memory_space=pltpu.MemorySpace.HBM)
SMEM = pl.BlockSpec(memory_space=pltpu.SMEM)
PARAMS = pltpu.CompilerParams(vmem_limit_bytes=12 * 1024 * 1024)


def partial_kernel(place_ref, x_ref, g0_ref, u0_ref, g1_ref, u1_ref, keep_ref, send_ref):
    half, core = place_ref[0], place_ref[1]
    count, ff = x_ref.shape[1], g0_ref.shape[1]

    def rows_of(b):
        return jnp.concatenate([x_ref[2 * (1 - half) + b], x_ref[2 * half + b]], axis=0)

    near, far = rows_of(core), rows_of(1 - core)
    for k, (w0, w1) in enumerate(((g0_ref, g1_ref), (u0_ref, u1_ref))):
        total = jnp.dot(near, w0[...], preferred_element_type=F32)
        total = total + jnp.dot(far, w1[...], preferred_element_type=F32)
        send_ref[:, k * ff : (k + 1) * ff] = total[:count].astype(BF16)
        keep_ref[:, k * ff : (k + 1) * ff] = total[count:].astype(BF16)


def partial_gate_up(place, x, weights):
    count, ff = x.shape[1], weights[0].shape[1]
    flops = 2 * 4 * count * x.shape[2] * 2 * ff
    return pl.pallas_call(
        partial_kernel,
        out_shape=(
            jax.ShapeDtypeStruct((count, 2 * ff), BF16),
            jax.ShapeDtypeStruct((count, 2 * ff), BF16),
        ),
        in_specs=[SMEM] + [VMEM] * 5,
        out_specs=(VMEM, VMEM),
        compiler_params=PARAMS,
        cost_estimate=pl.CostEstimate(flops=flops, bytes_accessed=6 << 20, transcendentals=0),
        name="partial_gate_up",
    )(place, x, *weights)


def hidden_grad_kernel(keep_ref, other_ref, grad_ref, out_ref):
    ff = grad_ref.shape[1]
    gate = keep_ref[:, :ff].astype(F32) + other_ref[:, :ff].astype(F32)
    up = keep_ref[:, ff:].astype(F32) + other_ref[:, ff:].astype(F32)
    grad_out = grad_ref[...].astype(F32)
    sig = jax.nn.sigmoid(gate)
    out_ref[:, :ff] = (grad_out * up * sig * (1.0 + gate * (1.0 - sig))).astype(BF16)
    out_ref[:, ff:] = (grad_out * gate * sig).astype(BF16)


def hidden_grad(keep, other, grad):
    return pl.pallas_call(
        hidden_grad_kernel,
        out_shape=jax.ShapeDtypeStruct(keep.shape, BF16),
        in_specs=[VMEM] * 3,
        out_specs=VMEM,
        compiler_params=PARAMS,
        cost_estimate=pl.CostEstimate(flops=1 << 20, bytes_accessed=1 << 20, transcendentals=1 << 16),
        name="hidden_grad",
    )(keep, other, grad)


def input_grad_kernel(place_ref, d0_ref, d1_ref, g0_ref, u0_ref, g1_ref, u1_ref, out_ref):
    half, core = place_ref[0], place_ref[1]
    count, ff = d0_ref.shape[0], g0_ref.shape[1]
    dims = (((1,), (1,)), ((), ()))
    d = jnp.concatenate([d0_ref[...], d1_ref[...]], axis=0)
    for w_gate, w_up, b in ((g0_ref, u0_ref, core), (g1_ref, u1_ref, 1 - core)):
        total = lax.dot_general(d[:, :ff], w_gate[...], dims, preferred_element_type=F32)
        total = total + lax.dot_general(d[:, ff:], w_up[...], dims, preferred_element_type=F32)
        out_ref[2 * half + b] = total[:count].astype(BF16)
        out_ref[2 * (1 - half) + b] = total[count:].astype(BF16)


def input_grad(place, d_own, d_other, weights):
    (count, cols), rows = d_own.shape, weights[0].shape[0]
    flops = 2 * 4 * count * rows * cols
    return pl.pallas_call(
        input_grad_kernel,
        out_shape=jax.ShapeDtypeStruct((4, count, rows), BF16),
        in_specs=[SMEM] + [VMEM] * 6,
        out_specs=VMEM,
        compiler_params=PARAMS,
        cost_estimate=pl.CostEstimate(flops=flops, bytes_accessed=6 << 20, transcendentals=0),
        name="input_grad",
    )(place, d_own, d_other, *weights)


def weight_grad_rows(place_ref, x_ref, d_ref, x_held, d_held, x_sem, d_sem, other):
    half, core = place_ref[0], place_ref[1]
    b = 1 - core if other else core
    pairs = d_ref.shape[0]
    step = 256
    copies = [pltpu.make_async_copy(d_ref, d_held, d_sem.at[0])]
    for n in range(pairs):
        a = half if n % 2 == 0 else 1 - half
        copies.append(
            pltpu.make_async_copy(x_ref.at[4 * (n // 2) + 2 * a + b], x_held.at[n], x_sem.at[n])
        )
    for copy in copies:
        copy.start()
    for copy in copies:
        copy.wait()
    for i in range(0, x_held.shape[2], step):
        at = slice(i, i + step)
        yield at, lax.dot_general(
            x_held[:, :, at].reshape(-1, step),
            d_held[...].reshape(-1, d_held.shape[2]),
            (((0,), (0,)), ((), ())),
            preferred_element_type=F32,
        )


def weight_grad_other_kernel(place_ref, x_ref, d_ref, out_ref, *scratch):
    for at, total in weight_grad_rows(place_ref, x_ref, d_ref, *scratch, True):
        out_ref[at, :] = total.astype(BF16)


def weight_grad_own_kernel(place_ref, x_ref, d_ref, got_ref, gate_ref, up_ref, *scratch):
    ff = gate_ref.shape[1]
    *scratch, got_held, got_sem = scratch
    copy = pltpu.make_async_copy(got_ref, got_held, got_sem.at[0])
    copy.start()
    for at, total in weight_grad_rows(place_ref, x_ref, d_ref, *scratch, False):
        if at.start == 0:
            copy.wait()
        total = (total + got_held[at, :].astype(F32)).astype(BF16)
        gate_ref[at, :] = total[:, :ff]
        up_ref[at, :] = total[:, ff:]


def weight_grad(kernel, name, place, inputs, d, got, shapes):
    pairs, count, cols = d.shape
    rows = inputs.shape[2]
    flops = 2 * pairs * count * rows * cols
    return pl.pallas_call(
        kernel,
        out_shape=[jax.ShapeDtypeStruct(v, BF16) for v in shapes],
        in_specs=[SMEM, HBM, HBM] + [HBM] * len(got),
        out_specs=[VMEM] * len(shapes),
        scratch_shapes=[
            pltpu.VMEM((pairs, count, rows), BF16),
            pltpu.VMEM((pairs, count, cols), BF16),
            pltpu.SemaphoreType.DMA((pairs,)),
            pltpu.SemaphoreType.DMA((1,)),
        ]
        + [v for g in got for v in (pltpu.VMEM(g.shape, BF16), pltpu.SemaphoreType.DMA((1,)))],
        compiler_params=pltpu.CompilerParams(vmem_limit_bytes=62 * 1024 * 1024),
        cost_estimate=pl.CostEstimate(flops=flops, bytes_accessed=8 << 20, transcendentals=0),
        name=name,
    )(place, inputs, d, *got)


def shards(quantized, scales, d_hidden, w_gate, w_up):
    count, width = quantized.shape
    rows, ff = w_gate.shape
    place = jnp.stack([lax.axis_index("zh"), lax.axis_index("c"), lax.axis_index("x")]).astype(jnp.int32)
    local = (quantized.astype(F32) * scales).astype(BF16)
    with jax.named_scope("gather_inputs"):
        held = spread(swap_half_y(local), "zl")
        held = held.transpose(1, 0, 2).reshape(count, rows)
        inputs = spread(held, "y")
        inputs, *others = lax.optimization_barrier((inputs, swap_core(w_gate), swap_core(w_up)))
        weights = (w_gate, w_up, *others)
    with jax.named_scope("partial_gate_up"):
        keep, sent = partial_gate_up(place, inputs, weights)
        inputs, sent = lax.optimization_barrier((inputs, sent))
    with jax.named_scope("all_inputs"):
        all_inputs = lax.all_gather(inputs, "x", axis=0, tiled=True)
    with jax.named_scope("half_sum"):
        other = swap_half(sent)
    with jax.named_scope("hidden_grad"):
        d_own = hidden_grad(keep, other, d_hidden)
    with jax.named_scope("d_far"):
        d_far = swap_half(d_own)
    with jax.named_scope("d_input"):
        di = input_grad(place, d_own, d_far, weights)
        di, d_own, d_far = lax.optimization_barrier((di, d_own, d_far))
        di = jnp.sum(lax.all_to_all(di, "y", 0, 0).astype(F32), axis=0).astype(BF16)
        di = di.reshape(count, 8, width).transpose(1, 0, 2)
        di = lax.all_to_all(di, "zl", 0, 0)
    with jax.named_scope("d_over_x"):
        d_both, all_inputs = lax.optimization_barrier((jnp.stack([d_own, d_far]), all_inputs))
        d_all = lax.all_gather(d_both, "x", axis=0, tiled=True)
    with jax.named_scope("weight_grads"):
        (sent,) = weight_grad(
            weight_grad_other_kernel, "weight_grad_other", place, all_inputs, d_all, (), [(rows, 2 * ff)]
        )
        di, sent = lax.optimization_barrier((di, sent))
        d_gate_weight, d_up_weight = weight_grad(
            weight_grad_own_kernel,
            "weight_grad_own",
            place,
            all_inputs,
            d_all,
            (swap_core(sent),),
            [(rows, ff)] * 2,
        )
    with jax.named_scope("d_input"):
        di = swap_half_y(jnp.sum(di.astype(F32), axis=0).astype(BF16))
    return lax.optimization_barrier((di, d_gate_weight, d_up_weight))


def solution(mesh):
    fine = Mesh(mesh.devices.reshape([SIZES[a] for a in AXES]), AXES)
    in_specs = (P(ROWS, COLS), P(ROWS, COLS), P(ROWS, COLS), P(SHARD, COLS), P(SHARD, COLS))
    out_specs = (P(ROWS, COLS), P(SHARD, COLS), P(SHARD, COLS))
    return jax.shard_map(shards, mesh=fine, in_specs=in_specs, out_specs=out_specs, check_vma=False)
```

```python
import jax
import jax.numpy as jnp
import numpy as np
from jax import lax
from jax.experimental import pallas as pl
from jax.experimental.pallas import tpu as pltpu
from jax.sharding import Mesh, PartitionSpec as P

AXES = ("x", "zh", "c", "y", "zl")
SIZES = {"x": 4, "zh": 2, "c": 2, "y": 4, "zl": 8}
ROWS = ("x", "zh", "c")
COLS = ("y", "zl")
SHARD = ("zh", "c")
F32 = jnp.float32
BF16 = jnp.bfloat16


def permute(value, axes, target):
    sizes = [SIZES[a] for a in axes]
    pairs = []
    for i in range(int(np.prod(sizes))):
        at = dict(zip(axes, map(int, np.unravel_index(i, sizes))))
        to = target(at)
        pairs.append((i, int(np.ravel_multi_index([to[a] for a in axes], sizes))))
    return lax.ppermute(value, axes if len(axes) > 1 else axes[0], pairs)


def swap_half_y(value):
    return permute(
        value, ("zh", "y"), lambda d: {"zh": d["y"] // 2, "y": d["zh"] * 2 + d["y"] % 2}
    )


def swap_core(value):
    return permute(value, ("c",), lambda d: {"c": 1 - d["c"]})


def swap_half(value):
    return permute(value, ("zh",), lambda d: {"zh": 1 - d["zh"]})


def step_outer(value, k):
    return permute(value, ("x",), lambda d: {"x": (d["x"] + k) % 4})


def spread(value, axis):
    n = SIZES[axis]
    return lax.all_to_all(jnp.broadcast_to(value[None], (n,) + value.shape), axis, 0, 0)


VMEM = pl.BlockSpec(memory_space=pltpu.VMEM)
HBM = pl.BlockSpec(memory_space=pltpu.MemorySpace.HBM)
SMEM = pl.BlockSpec(memory_space=pltpu.SMEM)
PARAMS = pltpu.CompilerParams(vmem_limit_bytes=12 * 1024 * 1024)


def partial_kernel(place_ref, x_ref, g0_ref, u0_ref, g1_ref, u1_ref, keep_ref, send_ref):
    half, core = place_ref[0], place_ref[1]
    count, ff = x_ref.shape[1], g0_ref.shape[1]

    def rows_of(b):
        return jnp.concatenate([x_ref[2 * (1 - half) + b], x_ref[2 * half + b]], axis=0)

    near, far = rows_of(core), rows_of(1 - core)
    for k, (w0, w1) in enumerate(((g0_ref, g1_ref), (u0_ref, u1_ref))):
        total = jnp.dot(near, w0[...], preferred_element_type=F32)
        total = total + jnp.dot(far, w1[...], preferred_element_type=F32)
        send_ref[:, k * ff : (k + 1) * ff] = total[:count].astype(BF16)
        keep_ref[:, k * ff : (k + 1) * ff] = total[count:].astype(BF16)


def partial_gate_up(place, x, weights):
    count, ff = x.shape[1], weights[0].shape[1]
    flops = 2 * 4 * count * x.shape[2] * 2 * ff
    return pl.pallas_call(
        partial_kernel,
        out_shape=(
            jax.ShapeDtypeStruct((count, 2 * ff), BF16),
            jax.ShapeDtypeStruct((count, 2 * ff), BF16),
        ),
        in_specs=[SMEM] + [VMEM] * 5,
        out_specs=(VMEM, VMEM),
        compiler_params=PARAMS,
        cost_estimate=pl.CostEstimate(flops=flops, bytes_accessed=6 << 20, transcendentals=0),
        name="partial_gate_up",
    )(place, x, *weights)


def hidden_grad_kernel(keep_ref, other_ref, grad_ref, out_ref):
    ff = grad_ref.shape[1]
    gate = keep_ref[:, :ff].astype(F32) + other_ref[:, :ff].astype(F32)
    up = keep_ref[:, ff:].astype(F32) + other_ref[:, ff:].astype(F32)
    grad_out = grad_ref[...].astype(F32)
    sig = jax.nn.sigmoid(gate)
    out_ref[:, :ff] = (grad_out * up * sig * (1.0 + gate * (1.0 - sig))).astype(BF16)
    out_ref[:, ff:] = (grad_out * gate * sig).astype(BF16)


def hidden_grad(keep, other, grad):
    return pl.pallas_call(
        hidden_grad_kernel,
        out_shape=jax.ShapeDtypeStruct(keep.shape, BF16),
        in_specs=[VMEM] * 3,
        out_specs=VMEM,
        compiler_params=PARAMS,
        cost_estimate=pl.CostEstimate(flops=1 << 20, bytes_accessed=1 << 20, transcendentals=1 << 16),
        name="hidden_grad",
    )(keep, other, grad)


def input_grad_kernel(place_ref, d0_ref, d1_ref, g0_ref, u0_ref, g1_ref, u1_ref, out_ref):
    half, core = place_ref[0], place_ref[1]
    count, ff = d0_ref.shape[0], g0_ref.shape[1]
    dims = (((1,), (1,)), ((), ()))
    d = jnp.concatenate([d0_ref[...], d1_ref[...]], axis=0)
    for w_gate, w_up, b in ((g0_ref, u0_ref, core), (g1_ref, u1_ref, 1 - core)):
        total = lax.dot_general(d[:, :ff], w_gate[...], dims, preferred_element_type=F32)
        total = total + lax.dot_general(d[:, ff:], w_up[...], dims, preferred_element_type=F32)
        out_ref[2 * half + b] = total[:count].astype(BF16)
        out_ref[2 * (1 - half) + b] = total[count:].astype(BF16)


def input_grad(place, d_own, d_other, weights):
    (count, cols), rows = d_own.shape, weights[0].shape[0]
    flops = 2 * 4 * count * rows * cols
    return pl.pallas_call(
        input_grad_kernel,
        out_shape=jax.ShapeDtypeStruct((4, count, rows), BF16),
        in_specs=[SMEM] + [VMEM] * 6,
        out_specs=VMEM,
        compiler_params=PARAMS,
        cost_estimate=pl.CostEstimate(flops=flops, bytes_accessed=6 << 20, transcendentals=0),
        name="input_grad",
    )(place, d_own, d_other, *weights)


def add_parts_kernel(parts_ref, out_ref):
    width = out_ref.shape[2]
    for z in range(out_ref.shape[0]):
        total = parts_ref[0, :, z * width : (z + 1) * width].astype(F32)
        for y in range(1, parts_ref.shape[0]):
            total = total + parts_ref[y, :, z * width : (z + 1) * width].astype(F32)
        out_ref[z] = total.astype(BF16)


def add_parts(parts, width):
    _, count, rows = parts.shape
    return pl.pallas_call(
        add_parts_kernel,
        out_shape=jax.ShapeDtypeStruct((rows // width, count, width), BF16),
        in_specs=[VMEM],
        out_specs=VMEM,
        compiler_params=PARAMS,
        cost_estimate=pl.CostEstimate(flops=1 << 19, bytes_accessed=5 << 18, transcendentals=0),
        name="add_parts",
    )(parts)


STEP = 256


def weight_grad_kernel(
    place_ref, x_ref, d_ref, sent_ref, keep_ref, x_held, d_held, out_held, x_sem, d_sem, out_sem
):
    half, core = place_ref[0], place_ref[1]
    pairs = d_ref.shape[0]
    tokens = pltpu.make_async_copy(d_ref, d_held, d_sem.at[0])
    tokens.start()
    fetches = []
    for m in range(2):
        b = 1 - core if m == 0 else core
        for n in range(pairs):
            a = half if n % 2 == 0 else 1 - half
            fetches.append(
                pltpu.make_async_copy(
                    x_ref.at[4 * (n // 2) + 2 * a + b], x_held.at[m, n], x_sem.at[m, n]
                )
            )
    for fetch in fetches:
        fetch.start()
    tokens.wait()
    writes = []
    for m, out_ref in enumerate((sent_ref, keep_ref)):
        for fetch in fetches[m * pairs : (m + 1) * pairs]:
            fetch.wait()
        for i in range(out_ref.shape[0] // STEP):
            at = slice(i * STEP, (i + 1) * STEP)
            out_held[m, at, :] = lax.dot_general(
                x_held[m, :, :, at].reshape(-1, STEP),
                d_held[...].reshape(-1, d_held.shape[2]),
                (((0,), (0,)), ((), ())),
                preferred_element_type=F32,
            ).astype(BF16)
            write = pltpu.make_async_copy(
                out_held.at[m, pl.ds(i * STEP, STEP)],
                out_ref.at[pl.ds(i * STEP, STEP)],
                out_sem.at[m, i],
            )
            write.start()
            writes.append(write)
    for write in writes:
        write.wait()


def weight_grad(place, inputs, d):
    pairs, count, cols = d.shape
    rows = inputs.shape[2]
    flops = 2 * 2 * pairs * count * rows * cols
    return pl.pallas_call(
        weight_grad_kernel,
        out_shape=[jax.ShapeDtypeStruct((rows, cols), BF16)] * 2,
        in_specs=[SMEM, HBM, HBM],
        out_specs=[HBM, HBM],
        scratch_shapes=[
            pltpu.VMEM((2, pairs, count, rows), BF16),
            pltpu.VMEM((pairs, count, cols), BF16),
            pltpu.VMEM((2, rows, cols), BF16),
            pltpu.SemaphoreType.DMA((2, pairs)),
            pltpu.SemaphoreType.DMA((1,)),
            pltpu.SemaphoreType.DMA((2, rows // STEP)),
        ],
        compiler_params=pltpu.CompilerParams(vmem_limit_bytes=62 * 1024 * 1024),
        cost_estimate=pl.CostEstimate(flops=flops, bytes_accessed=10 << 20, transcendentals=0),
        name="weight_grad",
    )(place, inputs, d)


def shards(quantized, scales, d_hidden, w_gate, w_up):
    count, width = quantized.shape
    rows, ff = w_gate.shape
    place = jnp.stack([lax.axis_index("zh"), lax.axis_index("c"), lax.axis_index("x")]).astype(jnp.int32)
    local = (quantized.astype(F32) * scales).astype(BF16)
    with jax.named_scope("gather_inputs"):
        held = spread(swap_half_y(local), "zl")
        held = held.transpose(1, 0, 2).reshape(count, rows)
        inputs = spread(held, "y")
        inputs, *others = lax.optimization_barrier((inputs, swap_core(w_gate), swap_core(w_up)))
        weights = (w_gate, w_up, *others)
    with jax.named_scope("partial_gate_up"):
        keep, sent = partial_gate_up(place, inputs, weights)
        inputs, sent = lax.optimization_barrier((inputs, sent))
    with jax.named_scope("all_inputs"):
        all_inputs = lax.all_gather(inputs, "x", axis=0, tiled=True)
    with jax.named_scope("half_sum"):
        other = swap_half(sent)
    with jax.named_scope("hidden_grad"):
        d_own = hidden_grad(keep, other, d_hidden)
    with jax.named_scope("d_far"):
        d_far = swap_half(d_own)
    with jax.named_scope("d_input"):
        di = input_grad(place, d_own, d_far, weights)
        di, d_own, d_far = lax.optimization_barrier((di, d_own, d_far))
        di = add_parts(lax.all_to_all(di, "y", 0, 0), width)
        di = lax.all_to_all(di, "zl", 0, 0)
    with jax.named_scope("d_over_x"):
        d_both, all_inputs = lax.optimization_barrier((jnp.stack([d_own, d_far]), all_inputs))
        d_all = lax.all_gather(d_both, "x", axis=0, tiled=True)
    with jax.named_scope("weight_grads"):
        sent, keep = weight_grad(place, all_inputs, d_all)
        di, sent = lax.optimization_barrier((di, sent))
        got = swap_core(sent)
        d_gate_weight, d_up_weight = (
            (keep[:, k : k + ff].astype(F32) + got[:, k : k + ff].astype(F32)).astype(BF16) for k in (0, ff)
        )
    with jax.named_scope("d_input"):
        di = swap_half_y(jnp.sum(di.astype(F32), axis=0).astype(BF16))
    return lax.optimization_barrier((di, d_gate_weight, d_up_weight))


def solution(mesh):
    fine = Mesh(mesh.devices.reshape([SIZES[a] for a in AXES]), AXES)
    in_specs = (P(ROWS, COLS), P(ROWS, COLS), P(ROWS, COLS), P(SHARD, COLS), P(SHARD, COLS))
    out_specs = (P(ROWS, COLS), P(SHARD, COLS), P(SHARD, COLS))
    return jax.shard_map(shards, mesh=fine, in_specs=in_specs, out_specs=out_specs, check_vma=False)
```

```python
import jax
import jax.numpy as jnp
import numpy as np
from jax import lax
from jax.experimental import pallas as pl
from jax.experimental.pallas import tpu as pltpu
from jax.sharding import Mesh, PartitionSpec as P

AXES = ("x", "zh", "c", "y", "zl")
SIZES = {"x": 4, "zh": 2, "c": 2, "y": 4, "zl": 8}
ROWS = ("x", "zh", "c")
COLS = ("y", "zl")
SHARD = ("zh", "c")
F32 = jnp.float32
BF16 = jnp.bfloat16


def permute(value, axes, target):
    sizes = [SIZES[a] for a in axes]
    pairs = []
    for i in range(int(np.prod(sizes))):
        at = dict(zip(axes, map(int, np.unravel_index(i, sizes))))
        to = target(at)
        pairs.append((i, int(np.ravel_multi_index([to[a] for a in axes], sizes))))
    return lax.ppermute(value, axes if len(axes) > 1 else axes[0], pairs)


def swap_half_y(value):
    return permute(
        value, ("zh", "y"), lambda d: {"zh": d["y"] // 2, "y": d["zh"] * 2 + d["y"] % 2}
    )


def swap_core(value):
    return permute(value, ("c",), lambda d: {"c": 1 - d["c"]})


def swap_half(value):
    return permute(value, ("zh",), lambda d: {"zh": 1 - d["zh"]})


def step_outer(value, k):
    return permute(value, ("x",), lambda d: {"x": (d["x"] + k) % 4})


def spread(value, axis):
    n = SIZES[axis]
    return lax.all_to_all(jnp.broadcast_to(value[None], (n,) + value.shape), axis, 0, 0)


VMEM = pl.BlockSpec(memory_space=pltpu.VMEM)
HBM = pl.BlockSpec(memory_space=pltpu.MemorySpace.HBM)
SMEM = pl.BlockSpec(memory_space=pltpu.SMEM)
PARAMS = pltpu.CompilerParams(vmem_limit_bytes=12 * 1024 * 1024)


def partial_kernel(place_ref, x_ref, g0_ref, u0_ref, g1_ref, u1_ref, keep_ref, send_ref):
    half, core = place_ref[0], place_ref[1]
    count, ff = x_ref.shape[1], g0_ref.shape[1]

    def rows_of(b):
        return jnp.concatenate([x_ref[2 * (1 - half) + b], x_ref[2 * half + b]], axis=0)

    near, far = rows_of(core), rows_of(1 - core)
    for k, (w0, w1) in enumerate(((g0_ref, g1_ref), (u0_ref, u1_ref))):
        total = jnp.dot(near, w0[...], preferred_element_type=F32)
        total = total + jnp.dot(far, w1[...], preferred_element_type=F32)
        send_ref[:, k * ff : (k + 1) * ff] = total[:count].astype(BF16)
        keep_ref[:, k * ff : (k + 1) * ff] = total[count:].astype(BF16)


def partial_gate_up(place, x, weights):
    count, ff = x.shape[1], weights[0].shape[1]
    flops = 2 * 4 * count * x.shape[2] * 2 * ff
    return pl.pallas_call(
        partial_kernel,
        out_shape=(
            jax.ShapeDtypeStruct((count, 2 * ff), BF16),
            jax.ShapeDtypeStruct((count, 2 * ff), BF16),
        ),
        in_specs=[SMEM] + [VMEM] * 5,
        out_specs=(VMEM, VMEM),
        compiler_params=PARAMS,
        cost_estimate=pl.CostEstimate(flops=flops, bytes_accessed=6 << 20, transcendentals=0),
        name="partial_gate_up",
    )(place, x, *weights)


def hidden_grad_kernel(keep_ref, other_ref, grad_ref, out_ref):
    ff = grad_ref.shape[1]
    gate = keep_ref[:, :ff].astype(F32) + other_ref[:, :ff].astype(F32)
    up = keep_ref[:, ff:].astype(F32) + other_ref[:, ff:].astype(F32)
    grad_out = grad_ref[...].astype(F32)
    sig = jax.nn.sigmoid(gate)
    out_ref[:, :ff] = (grad_out * up * sig * (1.0 + gate * (1.0 - sig))).astype(BF16)
    out_ref[:, ff:] = (grad_out * gate * sig).astype(BF16)


def hidden_grad(keep, other, grad):
    return pl.pallas_call(
        hidden_grad_kernel,
        out_shape=jax.ShapeDtypeStruct(keep.shape, BF16),
        in_specs=[VMEM] * 3,
        out_specs=VMEM,
        compiler_params=PARAMS,
        cost_estimate=pl.CostEstimate(flops=1 << 20, bytes_accessed=1 << 20, transcendentals=1 << 16),
        name="hidden_grad",
    )(keep, other, grad)


def input_grad_kernel(place_ref, d0_ref, d1_ref, g0_ref, u0_ref, g1_ref, u1_ref, out_ref):
    half, core = place_ref[0], place_ref[1]
    count, ff = d0_ref.shape[0], g0_ref.shape[1]
    dims = (((1,), (1,)), ((), ()))
    d = jnp.concatenate([d0_ref[...], d1_ref[...]], axis=0)
    for w_gate, w_up, b in ((g0_ref, u0_ref, core), (g1_ref, u1_ref, 1 - core)):
        total = lax.dot_general(d[:, :ff], w_gate[...], dims, preferred_element_type=F32)
        total = total + lax.dot_general(d[:, ff:], w_up[...], dims, preferred_element_type=F32)
        out_ref[2 * half + b] = total[:count].astype(BF16)
        out_ref[2 * (1 - half) + b] = total[count:].astype(BF16)


def input_grad(place, d_own, d_other, weights):
    (count, cols), rows = d_own.shape, weights[0].shape[0]
    flops = 2 * 4 * count * rows * cols
    return pl.pallas_call(
        input_grad_kernel,
        out_shape=jax.ShapeDtypeStruct((4, count, rows), BF16),
        in_specs=[SMEM] + [VMEM] * 6,
        out_specs=VMEM,
        compiler_params=PARAMS,
        cost_estimate=pl.CostEstimate(flops=flops, bytes_accessed=6 << 20, transcendentals=0),
        name="input_grad",
    )(place, d_own, d_other, *weights)


def add_parts_kernel(parts_ref, out_ref):
    width = out_ref.shape[2]
    for z in range(out_ref.shape[0]):
        total = parts_ref[0, :, z * width : (z + 1) * width].astype(F32)
        for y in range(1, parts_ref.shape[0]):
            total = total + parts_ref[y, :, z * width : (z + 1) * width].astype(F32)
        out_ref[z] = total.astype(BF16)


def add_parts(parts, width):
    _, count, rows = parts.shape
    return pl.pallas_call(
        add_parts_kernel,
        out_shape=jax.ShapeDtypeStruct((rows // width, count, width), BF16),
        in_specs=[VMEM],
        out_specs=VMEM,
        compiler_params=PARAMS,
        cost_estimate=pl.CostEstimate(flops=1 << 19, bytes_accessed=5 << 18, transcendentals=0),
        name="add_parts",
    )(parts)


STEP = 256


def weight_grad_kernel(
    place_ref, x_ref, d_ref, sent_ref, keep_ref, x_held, d_held, out_held, x_sem, d_sem, out_sem
):
    half, core = place_ref[0], place_ref[1]
    pairs = d_ref.shape[0]
    tokens = pltpu.make_async_copy(d_ref, d_held, d_sem.at[0])
    tokens.start()
    fetches = []
    for m in range(2):
        b = 1 - core if m == 0 else core
        for n in range(pairs):
            a = half if n % 2 == 0 else 1 - half
            fetches.append(
                pltpu.make_async_copy(
                    x_ref.at[4 * (n // 2) + 2 * a + b], x_held.at[m, n], x_sem.at[m, n]
                )
            )
    for fetch in fetches:
        fetch.start()
    tokens.wait()
    writes = []
    for m, out_ref in enumerate((sent_ref, keep_ref)):
        for fetch in fetches[m * pairs : (m + 1) * pairs]:
            fetch.wait()
        for i in range(out_ref.shape[0] // STEP):
            at = slice(i * STEP, (i + 1) * STEP)
            out_held[m, at, :] = lax.dot_general(
                x_held[m, :, :, at].reshape(-1, STEP),
                d_held[...].reshape(-1, d_held.shape[2]),
                (((0,), (0,)), ((), ())),
                preferred_element_type=F32,
            ).astype(BF16)
            write = pltpu.make_async_copy(
                out_held.at[m, pl.ds(i * STEP, STEP)],
                out_ref.at[pl.ds(i * STEP, STEP)],
                out_sem.at[m, i],
            )
            write.start()
            writes.append(write)
    for write in writes:
        write.wait()


def weight_grad(place, inputs, d):
    pairs, count, cols = d.shape
    rows = inputs.shape[2]
    flops = 2 * 2 * pairs * count * rows * cols
    return pl.pallas_call(
        weight_grad_kernel,
        out_shape=[jax.ShapeDtypeStruct((rows, cols), BF16)] * 2,
        in_specs=[SMEM, HBM, HBM],
        out_specs=[HBM, HBM],
        scratch_shapes=[
            pltpu.VMEM((2, pairs, count, rows), BF16),
            pltpu.VMEM((pairs, count, cols), BF16),
            pltpu.VMEM((2, rows, cols), BF16),
            pltpu.SemaphoreType.DMA((2, pairs)),
            pltpu.SemaphoreType.DMA((1,)),
            pltpu.SemaphoreType.DMA((2, rows // STEP)),
        ],
        compiler_params=pltpu.CompilerParams(vmem_limit_bytes=62 * 1024 * 1024),
        cost_estimate=pl.CostEstimate(flops=flops, bytes_accessed=10 << 20, transcendentals=0),
        name="weight_grad",
    )(place, inputs, d)


def shards(quantized, scales, d_hidden, w_gate, w_up):
    count, width = quantized.shape
    rows, ff = w_gate.shape
    place = jnp.stack([lax.axis_index("zh"), lax.axis_index("c"), lax.axis_index("x")]).astype(jnp.int32)
    local = (quantized.astype(F32) * scales).astype(BF16)
    with jax.named_scope("gather_inputs"):
        held = spread(swap_half_y(local), "zl")
        held = held.transpose(1, 0, 2).reshape(count, rows)
        inputs = spread(held, "y")
        inputs, *others = lax.optimization_barrier((inputs, swap_core(w_gate), swap_core(w_up)))
        weights = (w_gate, w_up, *others)
    with jax.named_scope("partial_gate_up"):
        keep, sent = partial_gate_up(place, inputs, weights)
        inputs, sent = lax.optimization_barrier((inputs, sent))
    with jax.named_scope("all_inputs"):
        all_inputs = lax.all_gather(inputs, "x", axis=0, tiled=True)
    with jax.named_scope("half_sum"):
        other = swap_half(sent)
    with jax.named_scope("hidden_grad"):
        d_own = hidden_grad(keep, other, d_hidden)
    with jax.named_scope("d_far"):
        d_far = swap_half(d_own)
    with jax.named_scope("d_input"):
        di = input_grad(place, d_own, d_far, weights)
        di = add_parts(lax.all_to_all(di, "y", 0, 0), width)
        di = lax.all_to_all(di, "zl", 0, 0)
    with jax.named_scope("d_over_x"):
        d_both, all_inputs = lax.optimization_barrier((jnp.stack([d_own, d_far]), all_inputs))
        d_all = lax.all_gather(d_both, "x", axis=0, tiled=True)
    with jax.named_scope("weight_grads"):
        sent, keep = weight_grad(place, all_inputs, d_all)
        di, sent = lax.optimization_barrier((di, sent))
        got = swap_core(sent)
        d_gate_weight, d_up_weight = (
            (keep[:, k : k + ff].astype(F32) + got[:, k : k + ff].astype(F32)).astype(BF16) for k in (0, ff)
        )
    with jax.named_scope("d_input"):
        di = swap_half_y(jnp.sum(di.astype(F32), axis=0).astype(BF16))
    return lax.optimization_barrier((di, d_gate_weight, d_up_weight))


def solution(mesh):
    fine = Mesh(mesh.devices.reshape([SIZES[a] for a in AXES]), AXES)
    in_specs = (P(ROWS, COLS), P(ROWS, COLS), P(ROWS, COLS), P(SHARD, COLS), P(SHARD, COLS))
    out_specs = (P(ROWS, COLS), P(SHARD, COLS), P(SHARD, COLS))
    return jax.shard_map(shards, mesh=fine, in_specs=in_specs, out_specs=out_specs, check_vma=False)
```

```python
import jax
import jax.numpy as jnp
import numpy as np
from jax import lax
from jax.experimental import pallas as pl
from jax.experimental.pallas import tpu as pltpu
from jax.sharding import Mesh, PartitionSpec as P

AXES = ("x", "zh", "c", "y", "zl")
SIZES = {"x": 4, "zh": 2, "c": 2, "y": 4, "zl": 8}
ROWS = ("x", "zh", "c")
COLS = ("y", "zl")
SHARD = ("zh", "c")
F32 = jnp.float32
BF16 = jnp.bfloat16


def permute(value, axes, target):
    sizes = [SIZES[a] for a in axes]
    pairs = []
    for i in range(int(np.prod(sizes))):
        at = dict(zip(axes, map(int, np.unravel_index(i, sizes))))
        to = target(at)
        pairs.append((i, int(np.ravel_multi_index([to[a] for a in axes], sizes))))
    return lax.ppermute(value, axes if len(axes) > 1 else axes[0], pairs)


def swap_half_y(value):
    return permute(
        value, ("zh", "y"), lambda d: {"zh": d["y"] // 2, "y": d["zh"] * 2 + d["y"] % 2}
    )


def swap_core(value):
    return permute(value, ("c",), lambda d: {"c": 1 - d["c"]})


def swap_half(value):
    return permute(value, ("zh",), lambda d: {"zh": 1 - d["zh"]})


def step_outer(value, k):
    return permute(value, ("x",), lambda d: {"x": (d["x"] + k) % 4})


def spread(value, axis):
    n = SIZES[axis]
    return lax.all_to_all(jnp.broadcast_to(value[None], (n,) + value.shape), axis, 0, 0)


VMEM = pl.BlockSpec(memory_space=pltpu.VMEM)
HBM = pl.BlockSpec(memory_space=pltpu.MemorySpace.HBM)
SMEM = pl.BlockSpec(memory_space=pltpu.SMEM)
PARAMS = pltpu.CompilerParams(vmem_limit_bytes=12 * 1024 * 1024)


def partial_kernel(place_ref, x_ref, g0_ref, u0_ref, g1_ref, u1_ref, keep_ref, send_ref):
    half, core = place_ref[0], place_ref[1]
    count, ff = x_ref.shape[1], g0_ref.shape[1]

    def rows_of(b):
        return jnp.concatenate([x_ref[2 * (1 - half) + b], x_ref[2 * half + b]], axis=0)

    near, far = rows_of(core), rows_of(1 - core)
    for k, (w0, w1) in enumerate(((g0_ref, g1_ref), (u0_ref, u1_ref))):
        total = jnp.dot(near, w0[...], preferred_element_type=F32)
        total = total + jnp.dot(far, w1[...], preferred_element_type=F32)
        send_ref[:, k * ff : (k + 1) * ff] = total[:count].astype(BF16)
        keep_ref[:, k * ff : (k + 1) * ff] = total[count:].astype(BF16)


def partial_gate_up(place, x, weights):
    count, ff = x.shape[1], weights[0].shape[1]
    flops = 2 * 4 * count * x.shape[2] * 2 * ff
    return pl.pallas_call(
        partial_kernel,
        out_shape=(
            jax.ShapeDtypeStruct((count, 2 * ff), BF16),
            jax.ShapeDtypeStruct((count, 2 * ff), BF16),
        ),
        in_specs=[SMEM] + [VMEM] * 5,
        out_specs=(VMEM, VMEM),
        compiler_params=PARAMS,
        cost_estimate=pl.CostEstimate(flops=flops, bytes_accessed=6 << 20, transcendentals=0),
        name="partial_gate_up",
    )(place, x, *weights)


def hidden_grad_kernel(keep_ref, other_ref, grad_ref, out_ref):
    ff = grad_ref.shape[1]
    gate = keep_ref[:, :ff].astype(F32) + other_ref[:, :ff].astype(F32)
    up = keep_ref[:, ff:].astype(F32) + other_ref[:, ff:].astype(F32)
    grad_out = grad_ref[...].astype(F32)
    sig = jax.nn.sigmoid(gate)
    out_ref[:, :ff] = (grad_out * up * sig * (1.0 + gate * (1.0 - sig))).astype(BF16)
    out_ref[:, ff:] = (grad_out * gate * sig).astype(BF16)


def hidden_grad(keep, other, grad):
    return pl.pallas_call(
        hidden_grad_kernel,
        out_shape=jax.ShapeDtypeStruct(keep.shape, BF16),
        in_specs=[VMEM] * 3,
        out_specs=VMEM,
        compiler_params=PARAMS,
        cost_estimate=pl.CostEstimate(flops=1 << 20, bytes_accessed=1 << 20, transcendentals=1 << 16),
        name="hidden_grad",
    )(keep, other, grad)


def input_grad_kernel(place_ref, d0_ref, d1_ref, g0_ref, u0_ref, g1_ref, u1_ref, out_ref):
    half, core = place_ref[0], place_ref[1]
    count, ff = d0_ref.shape[0], g0_ref.shape[1]
    dims = (((1,), (1,)), ((), ()))
    d = jnp.concatenate([d0_ref[...], d1_ref[...]], axis=0)
    for w_gate, w_up, b in ((g0_ref, u0_ref, core), (g1_ref, u1_ref, 1 - core)):
        total = lax.dot_general(d[:, :ff], w_gate[...], dims, preferred_element_type=F32)
        total = total + lax.dot_general(d[:, ff:], w_up[...], dims, preferred_element_type=F32)
        out_ref[2 * half + b] = total[:count].astype(BF16)
        out_ref[2 * (1 - half) + b] = total[count:].astype(BF16)


def input_grad(place, d_own, d_other, weights):
    (count, cols), rows = d_own.shape, weights[0].shape[0]
    flops = 2 * 4 * count * rows * cols
    return pl.pallas_call(
        input_grad_kernel,
        out_shape=jax.ShapeDtypeStruct((4, count, rows), BF16),
        in_specs=[SMEM] + [VMEM] * 6,
        out_specs=VMEM,
        compiler_params=PARAMS,
        cost_estimate=pl.CostEstimate(flops=flops, bytes_accessed=6 << 20, transcendentals=0),
        name="input_grad",
    )(place, d_own, d_other, *weights)


def add_parts_kernel(parts_ref, out_ref):
    width = out_ref.shape[2]
    for z in range(out_ref.shape[0]):
        total = parts_ref[0, :, z * width : (z + 1) * width].astype(F32)
        for y in range(1, parts_ref.shape[0]):
            total = total + parts_ref[y, :, z * width : (z + 1) * width].astype(F32)
        out_ref[z] = total.astype(BF16)


def add_parts(parts, width):
    _, count, rows = parts.shape
    return pl.pallas_call(
        add_parts_kernel,
        out_shape=jax.ShapeDtypeStruct((rows // width, count, width), BF16),
        in_specs=[VMEM],
        out_specs=VMEM,
        compiler_params=PARAMS,
        cost_estimate=pl.CostEstimate(flops=1 << 19, bytes_accessed=5 << 18, transcendentals=0),
        name="add_parts",
    )(parts)


STEP = 256


def weight_grad_kernel(
    place_ref, x_ref, d_ref, sent_ref, keep_ref, x_held, d_held, total_held, out_held, x_sem, d_sem, out_sem
):
    half, core = place_ref[0], place_ref[1]
    pairs = d_ref.shape[0]
    tokens = [pltpu.make_async_copy(d_ref.at[n], d_held.at[n], d_sem.at[n]) for n in range(pairs)]
    fetches = []
    for m in range(2):
        b = 1 - core if m == 0 else core
        for n in range(pairs):
            a = half if n % 2 == 0 else 1 - half
            fetches.append(
                pltpu.make_async_copy(
                    x_ref.at[4 * (n // 2) + 2 * a + b], x_held.at[m, n], x_sem.at[m, n]
                )
            )
    for n in range(pairs):
        tokens[n].start()
        fetches[n].start()
    for n in range(pairs):
        fetches[pairs + n].start()
    writes = []

    def product(m, first, last, at):
        return lax.dot_general(
            x_held[m, first:last, :, at].reshape(-1, STEP),
            d_held[first:last].reshape(-1, d_held.shape[2]),
            (((0,), (0,)), ((), ())),
            preferred_element_type=F32,
        )

    def write_out(m, i, out_ref, value):
        out_held[m, i * STEP : (i + 1) * STEP, :] = value.astype(BF16)
        write = pltpu.make_async_copy(
            out_held.at[m, pl.ds(i * STEP, STEP)], out_ref.at[pl.ds(i * STEP, STEP)], out_sem.at[m, i]
        )
        write.start()
        writes.append(write)

    tiles = [(i, slice(i * STEP, (i + 1) * STEP)) for i in range(sent_ref.shape[0] // STEP)]
    middle = pairs // 2
    for n in range(middle):
        tokens[n].wait()
        fetches[n].wait()
    for i, at in tiles:
        total_held[at, :] = product(0, 0, middle, at)
    for n in range(middle, pairs):
        tokens[n].wait()
        fetches[n].wait()
    for i, at in tiles:
        write_out(0, i, sent_ref, total_held[at, :] + product(0, middle, pairs, at))
    for n in range(pairs):
        fetches[pairs + n].wait()
    for i, at in tiles:
        write_out(1, i, keep_ref, product(1, 0, pairs, at))
    for write in writes:
        write.wait()


def weight_grad(place, inputs, d):
    pairs, count, cols = d.shape
    rows = inputs.shape[2]
    flops = 2 * 2 * pairs * count * rows * cols
    return pl.pallas_call(
        weight_grad_kernel,
        out_shape=[jax.ShapeDtypeStruct((rows, cols), BF16)] * 2,
        in_specs=[SMEM, HBM, HBM],
        out_specs=[HBM, HBM],
        scratch_shapes=[
            pltpu.VMEM((2, pairs, count, rows), BF16),
            pltpu.VMEM((pairs, count, cols), BF16),
            pltpu.VMEM((rows, cols), F32),
            pltpu.VMEM((2, rows, cols), BF16),
            pltpu.SemaphoreType.DMA((2, pairs)),
            pltpu.SemaphoreType.DMA((pairs,)),
            pltpu.SemaphoreType.DMA((2, rows // STEP)),
        ],
        compiler_params=pltpu.CompilerParams(vmem_limit_bytes=62 * 1024 * 1024),
        cost_estimate=pl.CostEstimate(flops=flops, bytes_accessed=10 << 20, transcendentals=0),
        name="weight_grad",
    )(place, inputs, d)


def shards(quantized, scales, d_hidden, w_gate, w_up):
    count, width = quantized.shape
    rows, ff = w_gate.shape
    place = jnp.stack([lax.axis_index("zh"), lax.axis_index("c"), lax.axis_index("x")]).astype(jnp.int32)
    local = (quantized.astype(F32) * scales).astype(BF16)
    with jax.named_scope("gather_inputs"):
        held = spread(swap_half_y(local), "zl")
        held = held.transpose(1, 0, 2).reshape(count, rows)
        inputs = spread(held, "y")
        inputs, *others = lax.optimization_barrier((inputs, swap_core(w_gate), swap_core(w_up)))
        weights = (w_gate, w_up, *others)
    with jax.named_scope("partial_gate_up"):
        keep, sent = partial_gate_up(place, inputs, weights)
        inputs, sent = lax.optimization_barrier((inputs, sent))
    with jax.named_scope("all_inputs"):
        all_inputs = lax.all_gather(inputs, "x", axis=0, tiled=True)
    with jax.named_scope("half_sum"):
        other = swap_half(sent)
    with jax.named_scope("hidden_grad"):
        d_own = hidden_grad(keep, other, d_hidden)
    with jax.named_scope("d_far"):
        d_far = swap_half(d_own)
    with jax.named_scope("d_input"):
        di = input_grad(place, d_own, d_far, weights)
        di = add_parts(lax.all_to_all(di, "y", 0, 0), width)
        di = lax.all_to_all(di, "zl", 0, 0)
    with jax.named_scope("d_over_x"):
        d_both, all_inputs = lax.optimization_barrier((jnp.stack([d_own, d_far]), all_inputs))
        d_all = lax.all_gather(d_both, "x", axis=0, tiled=True)
    with jax.named_scope("weight_grads"):
        sent, keep = weight_grad(place, all_inputs, d_all)
        di, sent = lax.optimization_barrier((di, sent))
        got = swap_core(sent)
        d_gate_weight, d_up_weight = (
            (keep[:, k : k + ff].astype(F32) + got[:, k : k + ff].astype(F32)).astype(BF16) for k in (0, ff)
        )
    with jax.named_scope("d_input"):
        di = swap_half_y(jnp.sum(di.astype(F32), axis=0).astype(BF16))
    return lax.optimization_barrier((di, d_gate_weight, d_up_weight))


def solution(mesh):
    fine = Mesh(mesh.devices.reshape([SIZES[a] for a in AXES]), AXES)
    in_specs = (P(ROWS, COLS), P(ROWS, COLS), P(ROWS, COLS), P(SHARD, COLS), P(SHARD, COLS))
    out_specs = (P(ROWS, COLS), P(SHARD, COLS), P(SHARD, COLS))
    return jax.shard_map(shards, mesh=fine, in_specs=in_specs, out_specs=out_specs, check_vma=False)
```

```python
import jax
import jax.numpy as jnp
import numpy as np
from jax import lax
from jax.experimental import pallas as pl
from jax.experimental.pallas import tpu as pltpu
from jax.sharding import Mesh, PartitionSpec as P

AXES = ("x", "zh", "c", "y", "zl")
SIZES = {"x": 4, "zh": 2, "c": 2, "y": 4, "zl": 8}
ROWS = ("x", "zh", "c")
COLS = ("y", "zl")
SHARD = ("zh", "c")
F32 = jnp.float32
BF16 = jnp.bfloat16


def permute(value, axes, target):
    sizes = [SIZES[a] for a in axes]
    pairs = []
    for i in range(int(np.prod(sizes))):
        at = dict(zip(axes, map(int, np.unravel_index(i, sizes))))
        to = target(at)
        pairs.append((i, int(np.ravel_multi_index([to[a] for a in axes], sizes))))
    return lax.ppermute(value, axes if len(axes) > 1 else axes[0], pairs)


def swap_half_y(value):
    return permute(
        value, ("zh", "y"), lambda d: {"zh": d["y"] // 2, "y": d["zh"] * 2 + d["y"] % 2}
    )


def swap_core(value):
    return permute(value, ("c",), lambda d: {"c": 1 - d["c"]})


def swap_half(value):
    return permute(value, ("zh",), lambda d: {"zh": 1 - d["zh"]})


def step_outer(value, k):
    return permute(value, ("x",), lambda d: {"x": (d["x"] + k) % 4})


def spread(value, axis):
    n = SIZES[axis]
    return lax.all_to_all(jnp.broadcast_to(value[None], (n,) + value.shape), axis, 0, 0)


VMEM = pl.BlockSpec(memory_space=pltpu.VMEM)
HBM = pl.BlockSpec(memory_space=pltpu.MemorySpace.HBM)
SMEM = pl.BlockSpec(memory_space=pltpu.SMEM)
PARAMS = pltpu.CompilerParams(vmem_limit_bytes=12 * 1024 * 1024)


def partial_kernel(place_ref, x_ref, g0_ref, u0_ref, g1_ref, u1_ref, keep_ref, send_ref):
    half, core = place_ref[0], place_ref[1]
    count, ff = x_ref.shape[1], g0_ref.shape[1]

    def rows_of(b):
        return jnp.concatenate([x_ref[2 * (1 - half) + b], x_ref[2 * half + b]], axis=0)

    near, far = rows_of(core), rows_of(1 - core)
    for k, (w0, w1) in enumerate(((g0_ref, g1_ref), (u0_ref, u1_ref))):
        total = jnp.dot(near, w0[...], preferred_element_type=F32)
        total = total + jnp.dot(far, w1[...], preferred_element_type=F32)
        send_ref[:, k * ff : (k + 1) * ff] = total[:count].astype(BF16)
        keep_ref[:, k * ff : (k + 1) * ff] = total[count:].astype(BF16)


def partial_gate_up(place, x, weights):
    count, ff = x.shape[1], weights[0].shape[1]
    flops = 2 * 4 * count * x.shape[2] * 2 * ff
    return pl.pallas_call(
        partial_kernel,
        out_shape=(
            jax.ShapeDtypeStruct((count, 2 * ff), BF16),
            jax.ShapeDtypeStruct((count, 2 * ff), BF16),
        ),
        in_specs=[SMEM] + [VMEM] * 5,
        out_specs=(VMEM, VMEM),
        compiler_params=PARAMS,
        cost_estimate=pl.CostEstimate(flops=flops, bytes_accessed=6 << 20, transcendentals=0),
        name="partial_gate_up",
    )(place, x, *weights)


def hidden_grad_kernel(keep_ref, other_ref, grad_ref, out_ref):
    ff = grad_ref.shape[1]
    gate = keep_ref[:, :ff].astype(F32) + other_ref[:, :ff].astype(F32)
    up = keep_ref[:, ff:].astype(F32) + other_ref[:, ff:].astype(F32)
    grad_out = grad_ref[...].astype(F32)
    sig = jax.nn.sigmoid(gate)
    out_ref[:, :ff] = (grad_out * up * sig * (1.0 + gate * (1.0 - sig))).astype(BF16)
    out_ref[:, ff:] = (grad_out * gate * sig).astype(BF16)


def hidden_grad(keep, other, grad):
    return pl.pallas_call(
        hidden_grad_kernel,
        out_shape=jax.ShapeDtypeStruct(keep.shape, BF16),
        in_specs=[VMEM] * 3,
        out_specs=VMEM,
        compiler_params=PARAMS,
        cost_estimate=pl.CostEstimate(flops=1 << 20, bytes_accessed=1 << 20, transcendentals=1 << 16),
        name="hidden_grad",
    )(keep, other, grad)


def input_grad_kernel(place_ref, d0_ref, d1_ref, g0_ref, u0_ref, g1_ref, u1_ref, out_ref):
    half, core = place_ref[0], place_ref[1]
    count, ff = d0_ref.shape[0], g0_ref.shape[1]
    dims = (((1,), (1,)), ((), ()))
    d = jnp.concatenate([d0_ref[...], d1_ref[...]], axis=0)
    for w_gate, w_up, b in ((g0_ref, u0_ref, core), (g1_ref, u1_ref, 1 - core)):
        total = lax.dot_general(d[:, :ff], w_gate[...], dims, preferred_element_type=F32)
        total = total + lax.dot_general(d[:, ff:], w_up[...], dims, preferred_element_type=F32)
        out_ref[2 * half + b] = total[:count].astype(BF16)
        out_ref[2 * (1 - half) + b] = total[count:].astype(BF16)


def input_grad(place, d_own, d_other, weights):
    (count, cols), rows = d_own.shape, weights[0].shape[0]
    flops = 2 * 4 * count * rows * cols
    return pl.pallas_call(
        input_grad_kernel,
        out_shape=jax.ShapeDtypeStruct((4, count, rows), BF16),
        in_specs=[SMEM] + [VMEM] * 6,
        out_specs=VMEM,
        compiler_params=PARAMS,
        cost_estimate=pl.CostEstimate(flops=flops, bytes_accessed=6 << 20, transcendentals=0),
        name="input_grad",
    )(place, d_own, d_other, *weights)


def add_parts_kernel(parts_ref, out_ref):
    width = out_ref.shape[2]
    for z in range(out_ref.shape[0]):
        total = parts_ref[0, :, z * width : (z + 1) * width].astype(F32)
        for y in range(1, parts_ref.shape[0]):
            total = total + parts_ref[y, :, z * width : (z + 1) * width].astype(F32)
        out_ref[z] = total.astype(BF16)


def add_parts(parts, width):
    _, count, rows = parts.shape
    return pl.pallas_call(
        add_parts_kernel,
        out_shape=jax.ShapeDtypeStruct((rows // width, count, width), BF16),
        in_specs=[VMEM],
        out_specs=VMEM,
        compiler_params=PARAMS,
        cost_estimate=pl.CostEstimate(flops=1 << 19, bytes_accessed=5 << 18, transcendentals=0),
        name="add_parts",
    )(parts)


STEP = 512


def weight_grad_kernel(
    place_ref, x_ref, d_ref, sent_ref, keep_ref, x_held, d_held, total_held, out_held, x_sem, d_sem, out_sem
):
    half, core = place_ref[0], place_ref[1]
    pairs = d_ref.shape[0]
    tokens = [pltpu.make_async_copy(d_ref.at[n], d_held.at[n], d_sem.at[n]) for n in range(pairs)]
    fetches = []
    for m in range(2):
        b = 1 - core if m == 0 else core
        for n in range(pairs):
            a = half if n % 2 == 0 else 1 - half
            fetches.append(
                pltpu.make_async_copy(
                    x_ref.at[4 * (n // 2) + 2 * a + b], x_held.at[m, n], x_sem.at[m, n]
                )
            )
    for n in range(pairs):
        tokens[n].start()
        fetches[n].start()
    for n in range(pairs):
        fetches[pairs + n].start()
    writes = []

    def product(m, first, last, at):
        return lax.dot_general(
            x_held[m, first:last, :, at].reshape(-1, STEP),
            d_held[first:last].reshape(-1, d_held.shape[2]),
            (((0,), (0,)), ((), ())),
            preferred_element_type=F32,
        )

    def write_out(m, i, out_ref, value):
        out_held[m, i * STEP : (i + 1) * STEP, :] = value.astype(BF16)
        write = pltpu.make_async_copy(
            out_held.at[m, pl.ds(i * STEP, STEP)], out_ref.at[pl.ds(i * STEP, STEP)], out_sem.at[m, i]
        )
        write.start()
        writes.append(write)

    tiles = [(i, slice(i * STEP, (i + 1) * STEP)) for i in range(sent_ref.shape[0] // STEP)]
    middle = pairs // 2
    for n in range(middle):
        tokens[n].wait()
        fetches[n].wait()
    for i, at in tiles:
        total_held[at, :] = product(0, 0, middle, at)
    for n in range(middle, pairs):
        tokens[n].wait()
        fetches[n].wait()
    for i, at in tiles:
        write_out(0, i, sent_ref, total_held[at, :] + product(0, middle, pairs, at))
    for n in range(pairs):
        fetches[pairs + n].wait()
    for i, at in tiles:
        write_out(1, i, keep_ref, product(1, 0, pairs, at))
    for write in writes:
        write.wait()


def weight_grad(place, inputs, d):
    pairs, count, cols = d.shape
    rows = inputs.shape[2]
    flops = 2 * 2 * pairs * count * rows * cols
    return pl.pallas_call(
        weight_grad_kernel,
        out_shape=[jax.ShapeDtypeStruct((rows, cols), BF16)] * 2,
        in_specs=[SMEM, HBM, HBM],
        out_specs=[HBM, HBM],
        scratch_shapes=[
            pltpu.VMEM((2, pairs, count, rows), BF16),
            pltpu.VMEM((pairs, count, cols), BF16),
            pltpu.VMEM((rows, cols), F32),
            pltpu.VMEM((2, rows, cols), BF16),
            pltpu.SemaphoreType.DMA((2, pairs)),
            pltpu.SemaphoreType.DMA((pairs,)),
            pltpu.SemaphoreType.DMA((2, rows // STEP)),
        ],
        compiler_params=pltpu.CompilerParams(vmem_limit_bytes=62 * 1024 * 1024),
        cost_estimate=pl.CostEstimate(flops=flops, bytes_accessed=10 << 20, transcendentals=0),
        name="weight_grad",
    )(place, inputs, d)


def shards(quantized, scales, d_hidden, w_gate, w_up):
    count, width = quantized.shape
    rows, ff = w_gate.shape
    place = jnp.stack([lax.axis_index("zh"), lax.axis_index("c"), lax.axis_index("x")]).astype(jnp.int32)
    local = (quantized.astype(F32) * scales).astype(BF16)
    with jax.named_scope("gather_inputs"):
        held = spread(swap_half_y(local), "zl")
        held = held.transpose(1, 0, 2).reshape(count, rows)
        inputs = spread(held, "y")
        inputs, *others = lax.optimization_barrier((inputs, swap_core(w_gate), swap_core(w_up)))
        weights = (w_gate, w_up, *others)
    with jax.named_scope("partial_gate_up"):
        keep, sent = partial_gate_up(place, inputs, weights)
        inputs, sent = lax.optimization_barrier((inputs, sent))
    with jax.named_scope("all_inputs"):
        all_inputs = lax.all_gather(inputs, "x", axis=0, tiled=True)
    with jax.named_scope("half_sum"):
        other = swap_half(sent)
    with jax.named_scope("hidden_grad"):
        d_own = hidden_grad(keep, other, d_hidden)
    with jax.named_scope("d_far"):
        d_far = swap_half(d_own)
    with jax.named_scope("d_input"):
        di = input_grad(place, d_own, d_far, weights)
        di = add_parts(lax.all_to_all(di, "y", 0, 0), width)
        di = lax.all_to_all(di, "zl", 0, 0)
    with jax.named_scope("d_over_x"):
        d_both, all_inputs = lax.optimization_barrier((jnp.stack([d_own, d_far]), all_inputs))
        d_all = lax.all_gather(d_both, "x", axis=0, tiled=True)
    with jax.named_scope("weight_grads"):
        sent, keep = weight_grad(place, all_inputs, d_all)
        di, sent = lax.optimization_barrier((di, sent))
        got = swap_core(sent)
        d_gate_weight, d_up_weight = (
            (keep[:, k : k + ff].astype(F32) + got[:, k : k + ff].astype(F32)).astype(BF16) for k in (0, ff)
        )
    with jax.named_scope("d_input"):
        di = swap_half_y(jnp.sum(di.astype(F32), axis=0).astype(BF16))
    return lax.optimization_barrier((di, d_gate_weight, d_up_weight))


def solution(mesh):
    fine = Mesh(mesh.devices.reshape([SIZES[a] for a in AXES]), AXES)
    in_specs = (P(ROWS, COLS), P(ROWS, COLS), P(ROWS, COLS), P(SHARD, COLS), P(SHARD, COLS))
    out_specs = (P(ROWS, COLS), P(SHARD, COLS), P(SHARD, COLS))
    return jax.shard_map(shards, mesh=fine, in_specs=in_specs, out_specs=out_specs, check_vma=False)
```

```python
import jax
import jax.numpy as jnp
import numpy as np
from jax import lax
from jax.experimental import pallas as pl
from jax.experimental.pallas import tpu as pltpu
from jax.sharding import Mesh, PartitionSpec as P

AXES = ("x", "zh", "c", "y", "zl")
SIZES = {"x": 4, "zh": 2, "c": 2, "y": 4, "zl": 8}
ROWS = ("x", "zh", "c")
COLS = ("y", "zl")
SHARD = ("zh", "c")
F32 = jnp.float32
BF16 = jnp.bfloat16


def permute(value, axes, target):
    sizes = [SIZES[a] for a in axes]
    pairs = []
    for i in range(int(np.prod(sizes))):
        at = dict(zip(axes, map(int, np.unravel_index(i, sizes))))
        to = target(at)
        pairs.append((i, int(np.ravel_multi_index([to[a] for a in axes], sizes))))
    return lax.ppermute(value, axes if len(axes) > 1 else axes[0], pairs)


def swap_half_y(value):
    return permute(
        value, ("zh", "y"), lambda d: {"zh": d["y"] // 2, "y": d["zh"] * 2 + d["y"] % 2}
    )


def swap_core(value):
    return permute(value, ("c",), lambda d: {"c": 1 - d["c"]})


def swap_half(value):
    return permute(value, ("zh",), lambda d: {"zh": 1 - d["zh"]})


def step_outer(value, k):
    return permute(value, ("x",), lambda d: {"x": (d["x"] + k) % 4})


def spread(value, axis):
    n = SIZES[axis]
    return lax.all_to_all(jnp.broadcast_to(value[None], (n,) + value.shape), axis, 0, 0)


VMEM = pl.BlockSpec(memory_space=pltpu.VMEM)
HBM = pl.BlockSpec(memory_space=pltpu.MemorySpace.HBM)
SMEM = pl.BlockSpec(memory_space=pltpu.SMEM)
PARAMS = pltpu.CompilerParams(vmem_limit_bytes=12 * 1024 * 1024)


def partial_kernel(place_ref, x_ref, g0_ref, u0_ref, g1_ref, u1_ref, keep_ref, send_ref):
    half, core = place_ref[0], place_ref[1]
    count, ff = x_ref.shape[1], g0_ref.shape[1]

    def rows_of(b):
        return jnp.concatenate([x_ref[2 * (1 - half) + b], x_ref[2 * half + b]], axis=0)

    near, far = rows_of(core), rows_of(1 - core)
    for k, (w0, w1) in enumerate(((g0_ref, g1_ref), (u0_ref, u1_ref))):
        total = jnp.dot(near, w0[...], preferred_element_type=F32)
        total = total + jnp.dot(far, w1[...], preferred_element_type=F32)
        send_ref[:, k * ff : (k + 1) * ff] = total[:count].astype(BF16)
        keep_ref[:, k * ff : (k + 1) * ff] = total[count:].astype(BF16)


def partial_gate_up(place, x, weights):
    count, ff = x.shape[1], weights[0].shape[1]
    flops = 2 * 4 * count * x.shape[2] * 2 * ff
    return pl.pallas_call(
        partial_kernel,
        out_shape=(
            jax.ShapeDtypeStruct((count, 2 * ff), BF16),
            jax.ShapeDtypeStruct((count, 2 * ff), BF16),
        ),
        in_specs=[SMEM] + [VMEM] * 5,
        out_specs=(VMEM, VMEM),
        compiler_params=PARAMS,
        cost_estimate=pl.CostEstimate(flops=flops, bytes_accessed=6 << 20, transcendentals=0),
        name="partial_gate_up",
    )(place, x, *weights)


def hidden_grad_kernel(keep_ref, other_ref, grad_ref, out_ref):
    ff = grad_ref.shape[1]
    gate = keep_ref[:, :ff].astype(F32) + other_ref[:, :ff].astype(F32)
    up = keep_ref[:, ff:].astype(F32) + other_ref[:, ff:].astype(F32)
    grad_out = grad_ref[...].astype(F32)
    sig = jax.nn.sigmoid(gate)
    out_ref[:, :ff] = (grad_out * up * sig * (1.0 + gate * (1.0 - sig))).astype(BF16)
    out_ref[:, ff:] = (grad_out * gate * sig).astype(BF16)


def hidden_grad(keep, other, grad):
    return pl.pallas_call(
        hidden_grad_kernel,
        out_shape=jax.ShapeDtypeStruct(keep.shape, BF16),
        in_specs=[VMEM] * 3,
        out_specs=VMEM,
        compiler_params=PARAMS,
        cost_estimate=pl.CostEstimate(flops=1 << 20, bytes_accessed=1 << 20, transcendentals=1 << 16),
        name="hidden_grad",
    )(keep, other, grad)


def input_grad_kernel(place_ref, d0_ref, d1_ref, g0_ref, u0_ref, g1_ref, u1_ref, out_ref):
    half, core = place_ref[0], place_ref[1]
    count, ff = d0_ref.shape[0], g0_ref.shape[1]
    dims = (((1,), (1,)), ((), ()))
    d = jnp.concatenate([d0_ref[...], d1_ref[...]], axis=0)
    for w_gate, w_up, b in ((g0_ref, u0_ref, core), (g1_ref, u1_ref, 1 - core)):
        total = lax.dot_general(d[:, :ff], w_gate[...], dims, preferred_element_type=F32)
        total = total + lax.dot_general(d[:, ff:], w_up[...], dims, preferred_element_type=F32)
        out_ref[2 * half + b] = total[:count].astype(BF16)
        out_ref[2 * (1 - half) + b] = total[count:].astype(BF16)


def input_grad(place, d_own, d_other, weights):
    (count, cols), rows = d_own.shape, weights[0].shape[0]
    flops = 2 * 4 * count * rows * cols
    return pl.pallas_call(
        input_grad_kernel,
        out_shape=jax.ShapeDtypeStruct((4, count, rows), BF16),
        in_specs=[SMEM] + [VMEM] * 6,
        out_specs=VMEM,
        compiler_params=PARAMS,
        cost_estimate=pl.CostEstimate(flops=flops, bytes_accessed=6 << 20, transcendentals=0),
        name="input_grad",
    )(place, d_own, d_other, *weights)


def add_parts_kernel(parts_ref, out_ref):
    width = out_ref.shape[2]
    for z in range(out_ref.shape[0]):
        total = parts_ref[0, :, z * width : (z + 1) * width].astype(F32)
        for y in range(1, parts_ref.shape[0]):
            total = total + parts_ref[y, :, z * width : (z + 1) * width].astype(F32)
        out_ref[z] = total.astype(BF16)


def add_parts(parts, width):
    _, count, rows = parts.shape
    return pl.pallas_call(
        add_parts_kernel,
        out_shape=jax.ShapeDtypeStruct((rows // width, count, width), BF16),
        in_specs=[VMEM],
        out_specs=VMEM,
        compiler_params=PARAMS,
        cost_estimate=pl.CostEstimate(flops=1 << 19, bytes_accessed=5 << 18, transcendentals=0),
        name="add_parts",
    )(parts)


STEP = 256


def weight_grad_kernel(
    place_ref, x_ref, d_ref, sent_ref, keep_ref, x_held, d_held, total_held, out_held, x_sem, d_sem, out_sem
):
    half, core = place_ref[0], place_ref[1]
    pairs = d_ref.shape[0]
    tokens = [pltpu.make_async_copy(d_ref.at[n], d_held.at[n], d_sem.at[n]) for n in range(pairs)]
    fetches = []
    for m in range(2):
        b = 1 - core if m == 0 else core
        for n in range(pairs):
            a = half if n % 2 == 0 else 1 - half
            fetches.append(
                pltpu.make_async_copy(
                    x_ref.at[4 * (n // 2) + 2 * a + b], x_held.at[m, n], x_sem.at[m, n]
                )
            )
    for n in range(pairs):
        tokens[n].start()
        fetches[n].start()
    for n in range(pairs):
        fetches[pairs + n].start()
    writes = []

    def product(m, first, last, at):
        return lax.dot_general(
            x_held[m, first:last, :, at].reshape(-1, STEP),
            d_held[first:last].reshape(-1, d_held.shape[2]),
            (((0,), (0,)), ((), ())),
            preferred_element_type=F32,
        )

    def write_out(m, i, out_ref, value):
        out_held[m, i * STEP : (i + 1) * STEP, :] = value.astype(BF16)
        write = pltpu.make_async_copy(
            out_held.at[m, pl.ds(i * STEP, STEP)], out_ref.at[pl.ds(i * STEP, STEP)], out_sem.at[m, i]
        )
        write.start()
        writes.append(write)

    tiles = [(i, slice(i * STEP, (i + 1) * STEP)) for i in range(sent_ref.shape[0] // STEP)]
    middle = pairs // 2
    for n in range(middle):
        tokens[n].wait()
        fetches[n].wait()
    for i, at in tiles:
        total_held[at, :] = product(0, 0, middle, at)
    for n in range(middle, pairs):
        tokens[n].wait()
        fetches[n].wait()
    for i, at in tiles:
        write_out(0, i, sent_ref, total_held[at, :] + product(0, middle, pairs, at))
    for n in range(pairs):
        fetches[pairs + n].wait()
    for i, at in tiles:
        write_out(1, i, keep_ref, product(1, 0, pairs, at))
    for write in writes:
        write.wait()


def weight_grad(place, inputs, d):
    pairs, count, cols = d.shape
    rows = inputs.shape[2]
    flops = 2 * 2 * pairs * count * rows * cols
    return pl.pallas_call(
        weight_grad_kernel,
        out_shape=[jax.ShapeDtypeStruct((rows, cols), BF16)] * 2,
        in_specs=[SMEM, HBM, HBM],
        out_specs=[HBM, HBM],
        scratch_shapes=[
            pltpu.VMEM((2, pairs, count, rows), BF16),
            pltpu.VMEM((pairs, count, cols), BF16),
            pltpu.VMEM((rows, cols), F32),
            pltpu.VMEM((2, rows, cols), BF16),
            pltpu.SemaphoreType.DMA((2, pairs)),
            pltpu.SemaphoreType.DMA((pairs,)),
            pltpu.SemaphoreType.DMA((2, rows // STEP)),
        ],
        compiler_params=pltpu.CompilerParams(vmem_limit_bytes=62 * 1024 * 1024),
        cost_estimate=pl.CostEstimate(flops=flops, bytes_accessed=10 << 20, transcendentals=0),
        name="weight_grad",
    )(place, inputs, d)


def shards(quantized, scales, d_hidden, w_gate, w_up):
    count, width = quantized.shape
    rows, ff = w_gate.shape
    place = jnp.stack([lax.axis_index("zh"), lax.axis_index("c"), lax.axis_index("x")]).astype(jnp.int32)
    local = (quantized.astype(F32) * scales).astype(BF16)
    with jax.named_scope("gather_inputs"):
        held = spread(swap_half_y(local), "zl")
        held = held.transpose(1, 0, 2).reshape(count, rows)
        inputs = spread(held, "y")
        inputs, *others = lax.optimization_barrier((inputs, swap_core(w_gate), swap_core(w_up)))
        weights = (w_gate, w_up, *others)
    with jax.named_scope("partial_gate_up"):
        keep, sent = partial_gate_up(place, inputs, weights)
        inputs, sent = lax.optimization_barrier((inputs, sent))
    with jax.named_scope("all_inputs"):
        all_inputs = lax.all_gather(inputs, "x", axis=0, tiled=True)
    with jax.named_scope("half_sum"):
        other = swap_half(sent)
    with jax.named_scope("hidden_grad"):
        d_own = hidden_grad(keep, other, d_hidden)
    with jax.named_scope("d_far"):
        d_far = swap_half(d_own)
    with jax.named_scope("d_input"):
        di = input_grad(place, d_own, d_far, weights)
        di = add_parts(lax.all_to_all(di, "y", 0, 0), width)
        di = lax.all_to_all(di, "zl", 0, 0)
    with jax.named_scope("d_over_x"):
        d_both, all_inputs = lax.optimization_barrier((jnp.stack([d_own, d_far]), all_inputs))
        d_all = lax.all_gather(d_both, "x", axis=0, tiled=True)
    with jax.named_scope("weight_grads"):
        sent, keep = weight_grad(place, all_inputs, d_all)
        di, sent = lax.optimization_barrier((di, sent))
        got = swap_core(sent)
        d_gate_weight, d_up_weight = (
            keep[:, k : k + ff] + got[:, k : k + ff] for k in (0, ff)
        )
    with jax.named_scope("d_input"):
        di = swap_half_y(jnp.sum(di.astype(F32), axis=0).astype(BF16))
    return lax.optimization_barrier((di, d_gate_weight, d_up_weight))


def solution(mesh):
    fine = Mesh(mesh.devices.reshape([SIZES[a] for a in AXES]), AXES)
    in_specs = (P(ROWS, COLS), P(ROWS, COLS), P(ROWS, COLS), P(SHARD, COLS), P(SHARD, COLS))
    out_specs = (P(ROWS, COLS), P(SHARD, COLS), P(SHARD, COLS))
    return jax.shard_map(shards, mesh=fine, in_specs=in_specs, out_specs=out_specs, check_vma=False)
```
